128 devices in a mesh: dom: 64 (over x, z, y), rep: 2 (over core).
Axes of the slice: x: 4, y: 4, z: 4, core: 2. Of those that a mesh axis runs over, the one named last changes fastest.
Arguments:
- features: bfloat16 [524288, 128], P('dom', 'rep'), may hold values from -6 to 6
- weight_first: bfloat16 [128, 256], P(None, 'rep'), may hold values from -0.5 to 0.5
- weight_second: bfloat16 [256, 47], P('rep'), may hold values from -1.5 to 1.5
- labels: int32 [524288], P('dom'), may hold values from 0 to 46
- send_index: int32 [64, 64, 2], P('dom'), may hold values from -1 to 63, as said below
- tile_src: int32 [16384], P('dom'), may hold values from 0 to 191, as said below
- tile_dst: int32 [16384], P('dom'), may hold values from 0 to 63, as said below
- tile_values: bfloat16 [16384, 128, 128], P('dom'), may hold values from -0.25 to 0.25
Outputs:
- hidden: bfloat16 [524288, 256], P('dom', 'rep')
- grad_first: float32 [128, 256], P(None, 'rep')
- grad_second: float32 [256, 47], P('rep')
- loss: float32 [], replicated
The draws below stay inside these ranges and needn't reach their ends.
Inputs may be any that keep to these rules, and one draw needn't show every extreme that they name: `send_index`: entry [s, r, j] names a local row block of partition s read by partition r in slot j; -1 marks an empty slot; the used slots of a pair come first; no partition reads from itself; a partition reads at most 2 blocks from each other one, many pairs use fewer or none; one hub partition reads 2 blocks from every other one. `tile_src`: the first 64 tiles of each partition map its block b onto its block b; every other tile names an own block or a used slot; each used slot is named by at least one tile. `tile_dst`: the first 64 tiles of each partition have destinations 0 to 63 in order.
All inputs are finite; a program needn't handle non-finite values.
Results may differ from the reference program's by a relative error of at most 0.006.
Values may be sent and summed in bfloat16 or wider, within the bound.
A program may use at most 192 MiB of HBM per device.

```python
import jax
import jax.numpy as jnp
from jax import lax

F_IN = 128
HID = 256
CLASSES = 47
BLK = 128
NB = 64
S = 2
NT = 256
NODES = 524288
N_DOM = 64


def link_counts(key):
    base = jax.random.fold_in(key, 7)
    key_dense, key_light, key_hub = jax.random.split(base, 3)
    dense_link = jax.random.randint(key_dense, (N_DOM, N_DOM), 0, 4) == 0
    light_link = jax.random.randint(key_light, (N_DOM, N_DOM), 0, S // 2 + 1)
    link_count = jnp.where(dense_link, S, light_link)
    hub_device = jax.random.randint(key_hub, (), 0, N_DOM)
    columns = jnp.arange(N_DOM, dtype=jnp.int32)
    link_count = jnp.where(columns[None, :] == hub_device, S, link_count)
    link_count = jnp.where(columns[:, None] == columns[None, :], 0, link_count)
    return link_count.astype(jnp.int32)


def draw_send_index(key, part):
    link_count = link_counts(key)
    key_blocks = jax.random.fold_in(key, 13)
    blocks = jax.random.randint(key_blocks, (N_DOM, N_DOM, S), 0, NB)
    slot_pos = jnp.arange(S, dtype=jnp.int32)
    return jnp.where(slot_pos[None, None, :] < link_count[:, :, None], blocks, -1).astype(jnp.int32)


def tile_plan(key):
    link_count = link_counts(key)
    base = jax.random.fold_in(key, 17)
    key_local, key_target = jax.random.split(base, 2)
    tile_pos = jnp.arange(NT, dtype=jnp.int32)
    in_slot = (tile_pos >= NB) & (tile_pos < NB + N_DOM * S)
    slot_flat = jnp.clip(tile_pos - NB, 0, N_DOM * S - 1)
    sender = slot_flat // S
    slot_pos = slot_flat % S
    received = link_count.T[:, sender]
    is_live = in_slot[None, :] & (slot_pos[None, :] < received)
    local_pick = jax.random.randint(key_local, (N_DOM, NT), 0, NB)
    sources = jnp.where(tile_pos[None, :] < NB, tile_pos[None, :], jnp.where(is_live, NB + slot_flat[None, :], local_pick))
    target_pick = jax.random.randint(key_target, (N_DOM, NT), 0, NB)
    targets = jnp.where(tile_pos[None, :] < NB, tile_pos[None, :], target_pick)
    return (sources.reshape(-1).astype(jnp.int32), targets.reshape(-1).astype(jnp.int32))


def draw_tile_src(key, part):
    return tile_plan(key)[0]


def draw_tile_dst(key, part):
    return tile_plan(key)[1]


def touch_ends(drawn, stream_key, low, high):
    place = [jax.random.randint(jax.random.fold_in(stream_key, axis), (), 0, length) for axis, length in enumerate(drawn.shape)]
    longest = drawn.shape.index(max(drawn.shape))
    beside = place[:longest] + [(place[longest] + 1) % drawn.shape[longest]] + place[longest + 1:]
    return drawn.at[tuple(place)].set(low).at[tuple(beside)].set(high)


def level_of(rng, extent, pieces, smallest, top_value):
    level = 1.0
    for position, blocks in pieces:
        heights = jax.random.uniform(jax.random.fold_in(jax.random.fold_in(rng, 6), position), (blocks,), jnp.float32, smallest / len(pieces), top_value / len(pieces))
        level = level * jnp.repeat(jnp.exp(heights), extent[position] // blocks).reshape((-1,) + (1,) * (len(extent) - 1 - position))
    return level


def scatter_about(rng, dims, deviation, most, cuts=(), kind=jnp.bfloat16):
    entries = jax.random.normal(rng, dims, jnp.float32) * deviation
    if len(cuts) > 0:
        entries = level_of(rng, dims, cuts, -0.22, 0.18) * entries
    return jnp.clip(entries, min=-most, max=most).astype(kind)


def setup_inputs(seed: int = 0) -> dict:
    streams_of = jax.random.split(jax.random.key(seed), 9)
    features = scatter_about(streams_of[0], (NODES, F_IN), 1.0, 6.0, ((0, 64), (1, 2)))
    weight_first = scatter_about(streams_of[1], (F_IN, HID), F_IN ** -0.5, 0.5, ((1, 2),))
    weight_second = scatter_about(streams_of[2], (HID, CLASSES), (4.0 / HID ** 0.5), 1.5, ((0, 2),))
    labels = touch_ends(jax.random.randint(streams_of[3], (NODES,), 0, CLASSES), jax.random.fold_in(streams_of[3], 1), 0, CLASSES - 1).astype(jnp.int32)
    send_index = draw_send_index(jax.random.fold_in(streams_of[8], 71), 0)
    tile_src = draw_tile_src(jax.random.fold_in(streams_of[8], 71), 0)
    tile_dst = draw_tile_dst(jax.random.fold_in(streams_of[8], 71), 0)
    tile_values = scatter_about(streams_of[7], (N_DOM * NT, BLK, BLK), (BLK * NT // NB) ** -0.5, 0.25, ((0, 64),))
    return {"features": features, "weight_first": weight_first, "weight_second": weight_second, "labels": labels, "send_index": send_index, "tile_src": tile_src, "tile_dst": tile_dst, "tile_values": tile_values}


def build_table(blocks_all, send_index, device):
    slot_index = send_index[:, device, :]
    senders = jnp.arange(N_DOM, dtype=jnp.int32)[:, None]
    chosen = blocks_all[senders, jnp.clip(slot_index, 0, NB - 1)]
    chosen = jnp.where((slot_index >= 0)[:, :, None, None], chosen, jnp.zeros((), blocks_all.dtype))
    width_cols = blocks_all.shape[-1]
    return jnp.concatenate([blocks_all[device], chosen.reshape(N_DOM * S, BLK, width_cols)], axis=0)


def aggregate(block_table, sources, targets, tile_vals):
    gathered = block_table[sources].astype(jnp.float32)
    products = jnp.einsum('tij,tjw->tiw', tile_vals.astype(jnp.float32), gathered)
    summed = jax.ops.segment_sum(products, targets, num_segments=NB)
    return summed.reshape(NB * BLK, -1)


def reference(features, weight_first, weight_second, labels, send_index, tile_src, tile_dst, tile_values):
    sources = tile_src.reshape(N_DOM, NT)
    targets = tile_dst.reshape(N_DOM, NT)
    tile_vals = tile_values.reshape(N_DOM, NT, BLK, BLK)
    devices = jnp.arange(N_DOM, dtype=jnp.int32)
    node_count = N_DOM * NB * BLK

    feat_blocks = features.reshape(N_DOM, NB, BLK, F_IN)
    first_mixed = lax.map(lambda device: aggregate(build_table(feat_blocks, send_index, device), sources[device], targets[device], tile_vals[device]).astype(jnp.bfloat16), devices)
    first_mixed = first_mixed.reshape(node_count, F_IN)
    pre_act = jnp.dot(first_mixed, weight_first, preferred_element_type=jnp.float32)
    hidden = jnp.maximum(pre_act, 0.0).astype(jnp.bfloat16)

    hidden_blocks = hidden.reshape(N_DOM, NB, BLK, HID)
    second_mixed = lax.map(lambda device: aggregate(build_table(hidden_blocks, send_index, device), sources[device], targets[device], tile_vals[device]).astype(jnp.bfloat16), devices)
    second_mixed = second_mixed.reshape(node_count, HID)
    logits = jnp.dot(second_mixed, weight_second, preferred_element_type=jnp.float32)

    log_total = jnp.log(jnp.sum(jnp.exp(logits), axis=-1))
    onehot = (labels[:, None] == jnp.arange(CLASSES, dtype=jnp.int32)[None, :]).astype(jnp.float32)
    cross_ent = log_total - jnp.sum(logits * onehot, axis=-1)
    loss = jnp.sum(cross_ent) / node_count
    softmax_probs = jnp.exp(logits - log_total[:, None])
    grad_logits = ((softmax_probs - onehot) * (1.0 / (node_count ** 0.5))).astype(jnp.bfloat16)
    grad_second = jnp.dot(second_mixed.T, grad_logits, preferred_element_type=jnp.float32)
    grad_mixed = jnp.dot(grad_logits, weight_second.T, preferred_element_type=jnp.float32).astype(jnp.bfloat16)

    grad_blocks = grad_mixed.reshape(N_DOM, NB, BLK, HID)
    mixed_blocks = first_mixed.reshape(N_DOM, NB, BLK, F_IN)

    def add_device(accum_grad, device):
        picked = grad_blocks[device][targets[device]].astype(jnp.float32)
        products = jnp.einsum('tij,tiw->tjw', tile_vals[device].astype(jnp.float32), picked)
        partial_value = jax.ops.segment_sum(products, sources[device], num_segments=NB + N_DOM * S)
        mixed_table = build_table(mixed_blocks, send_index, device).astype(jnp.float32)
        hidden_table = build_table(hidden_blocks, send_index, device)
        masked = jnp.where(hidden_table > 0, partial_value, jnp.zeros((), jnp.float32))
        term = jnp.einsum('ebf,ebh->fh', mixed_table, masked, precision=lax.Precision.HIGHEST)
        return accum_grad + term, None

    grad_first, unused = lax.scan(add_device, jnp.zeros((F_IN, HID), jnp.float32), devices)
    return hidden, grad_first, grad_second, loss
```

```python
import functools

import jax
import jax.numpy as jnp
from jax import lax
from jax.experimental import pallas as pl
from jax.experimental.pallas import tpu as pltpu
from jax.sharding import PartitionSpec as P

MESH = pl.DeviceIdType.MESH
BLK = 128
NB = 64
HALF = NB // 2
S = 2
DOM = 64
NT = 256
ENTRIES = NB + DOM * S
CLS = 47
CPAD = 48
UNROLL = 4
LIST = NT + UNROLL
PAY = 192
PART = PAY // 4
VMEM_LIMIT = 48 << 20
F32 = jnp.float32
BF16 = jnp.bfloat16

VM = pl.BlockSpec(memory_space=pltpu.VMEM)
SM = pl.BlockSpec(memory_space=pltpu.SMEM)


def coords(dom):
    return dom // 16, (dom // 4) % 4, dom % 4


def shifted(dom, i, sign):
    x, z, y = coords(dom)
    dx, dz, dy = coords(i)
    return ((x + sign * dx + 4) % 4) * 16 + ((z + sign * dz + 4) % 4) * 4 + (y + sign * dy + 4) % 4


def shift_of(step):
    return (step * 22 - 1) % 63 + 1


def meet_all(dom, rep):
    barrier = pltpu.get_barrier_semaphore()

    @pl.loop(1, DOM)
    def _(i):
        pl.semaphore_signal(barrier, inc=1, device_id=(shifted(dom, i, 1), rep), device_id_type=MESH)

    pl.semaphore_signal(barrier, inc=1, device_id=(dom, 1 - rep), device_id_type=MESH)
    return lambda: pl.semaphore_wait(barrier, DOM)


def dot(a, b, dims):
    return lax.dot_general(a, b, (dims, ((), ())), preferred_element_type=F32)


NN = ((1,), (0,))
TN = ((0,), (0,))
NTR = ((1,), (1,))


def feature_kernel(pick, feat, w1, w2, table, w1_all, w2_all, outbox, inbox, other, wbox, wgot,
                   send_sem, recv_sem, fsend_sem, frecv_sem, side_send, side_recv):
    dom, rep = lax.axis_index("dom"), lax.axis_index("rep")
    sib = 1 - rep
    arrive = meet_all(dom, rep)

    @pl.loop(1, DOM)
    def _(step):
        i = shift_of(step)
        r = shifted(dom, i, 1)
        outbox[i] = jnp.concatenate([feat[pick[2 * r]], feat[pick[2 * r + 1]]], axis=1)

    w2_pad = jnp.concatenate([w2[...].astype(F32), jnp.zeros((BLK, BLK - CLS), F32)], axis=1)
    wbox[0] = w1[...]
    wbox[1] = w2_pad.T.astype(BF16)
    arrive()

    def main(i):
        return pltpu.make_async_remote_copy(
            src_ref=outbox.at[i], dst_ref=inbox.at[rep, dom], send_sem=send_sem.at[i], recv_sem=recv_sem.at[i],
            device_id=(shifted(dom, i, 1), rep), device_id_type=MESH)

    def pass_on(i):
        s = shifted(dom, i, -1)
        return pltpu.make_async_remote_copy(
            src_ref=inbox.at[rep, s], dst_ref=inbox.at[rep, s], send_sem=fsend_sem.at[i], recv_sem=frecv_sem.at[i],
            device_id=(dom, sib), device_id_type=MESH)

    def taken(i):
        s = shifted(dom, i, -1)
        return pltpu.make_async_remote_copy(
            src_ref=inbox.at[sib, s], dst_ref=inbox.at[sib, s], send_sem=fsend_sem.at[i], recv_sem=frecv_sem.at[i],
            device_id=(dom, sib), device_id_type=MESH)

    @pl.loop(1, DOM)
    def _(step):
        main(shift_of(step)).start()

    side = [
        pltpu.make_async_remote_copy(src_ref=feat, dst_ref=other, send_sem=side_send.at[0], recv_sem=side_recv.at[0],
                                     device_id=(dom, sib), device_id_type=MESH),
        pltpu.make_async_remote_copy(src_ref=wbox, dst_ref=wgot, send_sem=side_send.at[1], recv_sem=side_recv.at[1],
                                     device_id=(dom, sib), device_id_type=MESH),
    ]
    for c in side:
        c.start()
    for c in side:
        c.wait()
    w1_all[:, :BLK] = wbox[0]
    w1_all[:, BLK:] = wgot[0]
    w2_all[:, :BLK] = wbox[1][:CPAD]
    w2_all[:, BLK:] = wgot[1][:CPAD]

    @pl.loop(0, NB)
    def _(b):
        mine, yours = feat[b], other[b]
        table[b] = jnp.where(rep == 0, jnp.concatenate([mine, yours], axis=1), jnp.concatenate([yours, mine], axis=1))

    @pl.loop(1, DOM)
    def _(step):
        i = shift_of(step)
        main(i).wait_recv()
        pass_on(i).start()

    @pl.loop(1, DOM)
    def _(step):
        i = shift_of(step)
        taken(i).wait_recv()
        s = shifted(dom, i, -1)
        low, high = inbox[0, s], inbox[1, s]
        table[NB + 2 * s] = jnp.concatenate([low[:, :64], high[:, :64]], axis=1)
        table[NB + 2 * s + 1] = jnp.concatenate([low[:, 64:], high[:, 64:]], axis=1)

    @pl.loop(1, DOM)
    def _(step):
        i = shift_of(step)
        main(i).wait_send()
        pass_on(i).wait_send()


def exchange_features(pick, feat, w1, w2):
    return pl.pallas_call(
        feature_kernel,
        out_shape=(
            jax.ShapeDtypeStruct((ENTRIES, BLK, BLK), BF16),
            jax.ShapeDtypeStruct((BLK, 2 * BLK), BF16),
            jax.ShapeDtypeStruct((CPAD, 2 * BLK), BF16),
        ),
        in_specs=[SM, VM, VM, VM],
        out_specs=(VM, VM, VM),
        scratch_shapes=[
            pltpu.VMEM((DOM, BLK, BLK), BF16),
            pltpu.VMEM((2, DOM, BLK, BLK), BF16),
            pltpu.VMEM((NB, BLK, 64), BF16),
            pltpu.VMEM((2, BLK, BLK), BF16),
            pltpu.VMEM((2, BLK, BLK), BF16),
        ] + [pltpu.SemaphoreType.DMA((DOM,))] * 4 + [pltpu.SemaphoreType.DMA((2,))] * 2,
        compiler_params=pltpu.CompilerParams(collective_id=0, has_side_effects=True, vmem_limit_bytes=VMEM_LIMIT),
    )(pick, feat.reshape(NB, BLK, 64), w1, w2)


def build_list(src, dst, first, lists):
    def step(t, count):
        d = dst[t] - first
        lists[0, count] = t
        lists[1, count] = src[t]
        lists[2, count] = d
        return count + jnp.where((d >= 0) & (d < HALF), 1, 0)

    count = lax.fori_loop(NB, NT, step, 0)
    for u in range(UNROLL):
        lists[0, count + u] = 0
        lists[1, count + u] = 0
        lists[2, count + u] = HALF
    return (count + UNROLL - 1) // UNROLL


def gather_sum(groups, first, lists, tiles, table, acc):
    @pl.loop(0, HALF // UNROLL)
    def _(g):
        for u in range(UNROLL):
            b = g * UNROLL + u
            acc[b] = dot(tiles[first + b], table[first + b], NN)

    @pl.loop(0, groups)
    def _(g):
        at = [g * UNROLL + u for u in range(UNROLL)]
        products = [dot(tiles[lists[0, n]], table[lists[1, n]], NN) for n in at]
        for n, product in zip(at, products):
            acc[lists[2, n]] += product


def first_kernel(src, dst, tiles, table, mixed, acc, lists):
    first = lax.axis_index("rep") * HALF
    groups = build_list(src, dst, first, lists)
    gather_sum(groups, first, lists, tiles, table, acc)

    @pl.loop(0, HALF)
    def _(b):
        mixed[b] = acc[b].astype(BF16)


def first_aggregate(src, dst, tiles, table):
    return pl.pallas_call(
        first_kernel,
        out_shape=jax.ShapeDtypeStruct((HALF, BLK, BLK), BF16),
        in_specs=[SM, SM, VM, VM],
        out_specs=VM,
        scratch_shapes=[pltpu.VMEM((HALF + 1, BLK, BLK), F32), pltpu.SMEM((3, LIST), jnp.int32)],
        compiler_params=pltpu.CompilerParams(vmem_limit_bytes=VMEM_LIMIT),
    )(src, dst, tiles, table)


def mixed_kernel(pick, mixed, w1, table, hidden, own, outbox,
                 send_sem, recv_sem, fsend_sem, frecv_sem, side_send, side_recv):
    dom, rep = lax.axis_index("dom"), lax.axis_index("rep")
    sib = 1 - rep
    arrive = meet_all(dom, rep)

    @pl.loop(0, HALF)
    def _(b):
        own[rep * HALF + b] = mixed[b]

    arrive()
    side = pltpu.make_async_remote_copy(
        src_ref=mixed, dst_ref=own.at[pl.ds(rep * HALF, HALF)], send_sem=side_send, recv_sem=side_recv,
        device_id=(dom, sib), device_id_type=MESH)
    side.start()
    side.wait()

    def main(i):
        return pltpu.make_async_remote_copy(
            src_ref=outbox.at[i], dst_ref=table.at[NB + 2 * dom + rep], send_sem=send_sem.at[i],
            recv_sem=recv_sem.at[i], device_id=(shifted(dom, i, 1), rep), device_id_type=MESH)

    def pass_on(i):
        e = NB + 2 * shifted(dom, i, -1) + rep
        return pltpu.make_async_remote_copy(
            src_ref=table.at[e], dst_ref=table.at[e], send_sem=fsend_sem.at[i], recv_sem=frecv_sem.at[i],
            device_id=(dom, sib), device_id_type=MESH)

    def taken(i):
        e = NB + 2 * shifted(dom, i, -1) + sib
        return pltpu.make_async_remote_copy(
            src_ref=table.at[e], dst_ref=table.at[e], send_sem=fsend_sem.at[i], recv_sem=frecv_sem.at[i],
            device_id=(dom, sib), device_id_type=MESH)

    @pl.loop(1, DOM)
    def _(step):
        i = shift_of(step)
        outbox[i] = own[pick[2 * shifted(dom, i, 1) + rep]]
        main(i).start()

    def activate(e, rows):
        hidden[e] = jnp.maximum(dot(rows, w1[...], NN), 0.0).astype(BF16)

    @pl.loop(0, NB // 2)
    def _(g):
        for b in (2 * g, 2 * g + 1):
            table[b] = own[b]
            activate(b, own[b])

    @pl.loop(1, DOM)
    def _(step):
        i = shift_of(step)
        main(i).wait_recv()
        pass_on(i).start()
        e = NB + 2 * shifted(dom, i, -1) + rep
        activate(e, table[e])

    @pl.loop(1, DOM)
    def _(step):
        i = shift_of(step)
        taken(i).wait_recv()
        e = NB + 2 * shifted(dom, i, -1) + sib
        activate(e, table[e])

    @pl.loop(1, DOM)
    def _(step):
        i = shift_of(step)
        main(i).wait_send()
        pass_on(i).wait_send()


def exchange_mixed(pick, mixed, w1):
    return pl.pallas_call(
        mixed_kernel,
        out_shape=(
            jax.ShapeDtypeStruct((ENTRIES, BLK, BLK), BF16),
            jax.ShapeDtypeStruct((ENTRIES, BLK, 2 * BLK), BF16),
        ),
        in_specs=[SM, VM, VM],
        out_specs=(VM, VM),
        scratch_shapes=[pltpu.VMEM((NB, BLK, BLK), BF16), pltpu.VMEM((DOM, BLK, BLK), BF16)]
        + [pltpu.SemaphoreType.DMA((DOM,))] * 4 + [pltpu.SemaphoreType.DMA(())] * 2,
        compiler_params=pltpu.CompilerParams(collective_id=1, has_side_effects=True, vmem_limit_bytes=VMEM_LIMIT),
    )(pick, mixed, w1)


def second_kernel(scale, src, dst, labels, tiles, table, hidden, w2, pay, hidden_out, acc, grad, lists, sem):
    first = lax.axis_index("rep") * HALF
    out = pltpu.make_async_copy(hidden.at[pl.ds(0, NB), :, pl.ds(0, BLK)], hidden_out, sem)
    out.start()
    groups = build_list(src, dst, first, lists)
    gather_sum(groups, first, lists, tiles, hidden, acc)
    pay[...] = jnp.zeros_like(pay)
    grad[HALF] = jnp.zeros((BLK, 2 * BLK), BF16)
    w2_t = w2[...]
    kinds = lax.broadcasted_iota(jnp.int32, (CPAD, BLK), 0)

    def classify(b, loss):
        second = acc[b].astype(BF16)
        logits = dot(w2_t, second, NTR)
        powers = jnp.where(kinds < CLS, jnp.exp(logits), 0.0)
        total = jnp.sum(powers, axis=0, keepdims=True)
        hot = kinds == labels[b]
        loss = loss + jnp.log(total) - jnp.sum(jnp.where(hot, logits, 0.0), axis=0, keepdims=True)
        grad_logits = ((powers * (1.0 / total) - jnp.where(hot, 1.0, 0.0)) * scale).astype(BF16)
        pay[BLK:BLK + CPAD] += dot(grad_logits, second, NN)
        grad[b] = dot(grad_logits, w2_t, TN).astype(BF16)
        return loss

    def two(g, loss):
        return classify(2 * g + 1, classify(2 * g, loss))

    loss = lax.fori_loop(0, HALF // 2, two, jnp.zeros((1, BLK), F32))
    loss_sum = jnp.sum(loss)
    pay[BLK + CPAD:] = jnp.zeros((PAY - BLK - CPAD, 2 * BLK), F32) + loss_sum

    def back(t, e, d):
        part = dot(tiles[t], grad[d], TN)
        return jnp.where(hidden[e] > 0, part, 0.0).astype(BF16)

    def pair(a, b):
        rows = jnp.concatenate([table[a[1]], table[b[1]]], axis=0)
        return dot(rows, jnp.concatenate([back(*a), back(*b)], axis=0), TN)

    @pl.loop(0, HALF // UNROLL)
    def _(g):
        at = [g * UNROLL + u for u in range(UNROLL)]
        at = [(first + b, first + b, b) for b in at]
        pay[:BLK] += pair(at[0], at[1]) + pair(at[2], at[3])

    @pl.loop(0, groups)
    def _(g):
        at = [g * UNROLL + u for u in range(UNROLL)]
        at = [(lists[0, n], lists[1, n], lists[2, n]) for n in at]
        pay[:BLK] += pair(at[0], at[1]) + pair(at[2], at[3])

    out.wait()


def second_layer(scale, src, dst, labels, tiles, table, hidden, w2):
    return pl.pallas_call(
        functools.partial(second_kernel, scale),
        out_shape=(
            jax.ShapeDtypeStruct((PAY, 2 * BLK), F32),
            jax.ShapeDtypeStruct((NB, BLK, BLK), BF16),
        ),
        in_specs=[SM, SM, VM, VM, VM, VM, VM],
        out_specs=(VM, pl.BlockSpec(memory_space=pl.ANY)),
        scratch_shapes=[
            pltpu.VMEM((HALF + 1, BLK, 2 * BLK), F32),
            pltpu.VMEM((HALF + 1, BLK, 2 * BLK), BF16),
            pltpu.SMEM((3, LIST), jnp.int32),
            pltpu.SemaphoreType.DMA(()),
        ],
        compiler_params=pltpu.CompilerParams(vmem_limit_bytes=VMEM_LIMIT),
    )(src, dst, labels, tiles, table, hidden, w2)


def sum_kernel(pay, out, got, mine, parts, plane, psum, send_sem, recv_sem):
    dom, rep = lax.axis_index("dom"), lax.axis_index("rep")
    x, z, y = coords(dom)
    zy = z * 4 + y
    sib = 1 - rep

    def along_x(j):
        return ((x + j) % 4) * 16 + zy, (x + j) % 4

    def in_plane(j):
        return x * 16 + ((z + j // 4) % 4) * 4 + (y + j % 4) % 4

    barrier = pltpu.get_barrier_semaphore()
    pl.semaphore_signal(barrier, inc=1, device_id=(dom, sib), device_id_type=MESH)
    for j in range(1, 4):
        pl.semaphore_signal(barrier, inc=1, device_id=(along_x(j)[0], rep), device_id_type=MESH)
    for j in range(1, 16):
        pl.semaphore_signal(barrier, inc=1, device_id=(in_plane(j), rep), device_id_type=MESH)
    pl.semaphore_wait(barrier, 19)

    def copy(a, b, n, to):
        return pltpu.make_async_remote_copy(src_ref=a, dst_ref=b, send_sem=send_sem.at[n], recv_sem=recv_sem.at[n],
                                            device_id=to, device_id_type=MESH)

    side = copy(pay.at[:, pl.ds(BLK, BLK)], got, 0, (dom, sib))
    side.start()
    side.wait()
    mine[...] = pay[:, :BLK] + got[...]

    cut = []
    for j in range(1, 4):
        to, tx = along_x(j)
        cut.append(copy(mine.at[pl.ds(pl.multiple_of(tx * PART, 8), PART)], parts.at[j], j, (to, rep)))
        cut[-1].start()
    total = mine[pl.ds(pl.multiple_of(x * PART, 8), PART)]
    for j in range(1, 4):
        cut[j - 1].wait()
        total = total + parts[j]
    psum[...] = total

    across = []
    for j in range(1, 16):
        across.append(copy(psum, plane.at[j], 3 + j, (in_plane(j), rep)))
        across[-1].start()
    for j in range(1, 16):
        across[j - 1].wait()
    plane[0] = psum[...]
    total = plane[0]
    for j in range(1, 16):
        total = total + plane[j]
    here = pl.ds(pl.multiple_of(x * PART, 8), PART)
    out[here] = total

    back = []
    for j in range(1, 4):
        back.append(copy(out.at[here], out.at[here], 18 + j, (along_x(j)[0], rep)))
        back[-1].start()
    for c in back:
        c.wait_send()
    for j in range(1, 4):
        there = pl.ds(pl.multiple_of(((x + 4 - j) % 4) * PART, 8), PART)
        copy(out.at[there], out.at[there], 18 + j, (along_x(j)[0], rep)).wait_recv()


def sum_all(pay):
    return pl.pallas_call(
        sum_kernel,
        out_shape=jax.ShapeDtypeStruct((PAY, BLK), F32),
        in_specs=[VM],
        out_specs=VM,
        scratch_shapes=[
            pltpu.VMEM((PAY, BLK), F32),
            pltpu.VMEM((PAY, BLK), F32),
            pltpu.VMEM((4, PART, BLK), F32),
            pltpu.VMEM((16, PART, BLK), F32),
            pltpu.VMEM((PART, BLK), F32),
            pltpu.SemaphoreType.DMA((22,)),
            pltpu.SemaphoreType.DMA((22,)),
        ],
        compiler_params=pltpu.CompilerParams(collective_id=2, has_side_effects=True, vmem_limit_bytes=VMEM_LIMIT),
    )(pay)


def per_device(features, weight_first, weight_second, labels, send_index, tile_src, tile_dst, tile_values):
    node_count = lax.axis_size("dom") * NB * BLK
    pick = jnp.clip(send_index.reshape(-1), 0, NB - 1)
    table, w1, w2 = exchange_features(pick, features, weight_first, weight_second)
    mixed = first_aggregate(tile_src, tile_dst, tile_values, table)
    mixed_table, hidden = exchange_mixed(pick, mixed, w1)
    my_labels = lax.dynamic_slice(labels.reshape(NB, 1, BLK), (lax.axis_index("rep") * HALF, 0, 0), (HALF, 1, BLK))
    pay, hidden_out = second_layer(
        1.0 / node_count**0.5, tile_src, tile_dst, my_labels, tile_values, mixed_table, hidden, w2)
    total = sum_all(pay)
    grad_first = total[:BLK]
    grad_second = total[BLK:BLK + CLS].T
    loss = total[BLK + CPAD, 0] / node_count
    return hidden_out.reshape(NB * BLK, BLK), grad_first, grad_second, loss


def solution(mesh):
    return jax.shard_map(
        per_device,
        mesh=mesh,
        in_specs=(P("dom", "rep"), P(None, "rep"), P("rep", None), P("dom"), P("dom", None, None), P("dom"), P("dom"),
                  P("dom", None, None)),
        out_specs=(P("dom", "rep"), P(None, "rep"), P("rep", None), P()),
        check_vma=False,
    )
```

```python
import functools

import jax
import jax.numpy as jnp
from jax import lax
from jax.experimental import pallas as pl
from jax.experimental.pallas import tpu as pltpu
from jax.sharding import PartitionSpec as P

MESH = pl.DeviceIdType.MESH
BLK = 128
NB = 64
HALF = NB // 2
S = 2
DOM = 64
NT = 256
ENTRIES = NB + DOM * S
CLS = 47
CPAD = 48
UNROLL = 8
BATCH = 3
WIDE = 8
ROWS = WIDE * BLK
LIST = NT + UNROLL
PAY = 192
PART = PAY // 4
F32 = jnp.float32
BF16 = jnp.bfloat16

VM = pl.BlockSpec(memory_space=pltpu.VMEM)
SM = pl.BlockSpec(memory_space=pltpu.SMEM)
ANY = pl.BlockSpec(memory_space=pl.ANY)
COST = pl.CostEstimate(flops=10**10, bytes_accessed=10**8, transcendentals=0)


def coords(dom):
    return lax.div(dom, 16), lax.rem(lax.div(dom, 4), 4), lax.rem(dom, 4)


def shifted(dom, i, sign):
    x, z, y = coords(dom)
    dx, dz, dy = coords(i)
    return (lax.rem(x + sign * dx + 4, 4) * 16 + lax.rem(z + sign * dz + 4, 4) * 4 + lax.rem(y + sign * dy + 4, 4))


def shift_of(step):
    return lax.rem(step * 22 - 1, 63) + 1


def meet_all(dom, rep):
    barrier = pltpu.get_barrier_semaphore()
    pl.semaphore_signal(barrier, inc=1, device_id=(dom, 1 - rep), device_id_type=MESH)
    x, z, y = coords(dom)
    xs = [lax.rem(x + d, 4) * 16 for d in range(4)]
    zs = [lax.rem(z + d, 4) * 4 for d in range(4)]
    ys = [lax.rem(y + d, 4) for d in range(4)]
    for i in range(1, DOM):
        peer = xs[i // 16] + zs[i // 4 % 4] + ys[i % 4]
        pl.semaphore_signal(barrier, inc=1, device_id=(peer, rep), device_id_type=MESH)
    return lambda: pl.semaphore_wait(barrier, DOM)


def dot(a, b, dims):
    return lax.dot_general(a, b, (dims, ((), ())), preferred_element_type=F32)


NN = ((1,), (0,))
TN = ((0,), (0,))
NTR = ((1,), (1,))


def feature_kernel(pick, feat, table, blocks, outbox, send_sem, recv_sem, fsend_sem, frecv_sem, side_send, side_recv):
    dom, rep = lax.axis_index("dom"), lax.axis_index("rep")
    sib = 1 - rep
    arrive = meet_all(dom, rep)

    def half(k):
        return pl.ds(pl.multiple_of(k * 64, 64), 64)

    @pl.loop(0, NB)
    def _(b):
        blocks[b] = feat[:, pl.ds(pl.multiple_of(b * BLK, BLK), BLK)]

    @pl.loop(1, DOM)
    def _(step):
        i = shift_of(step)
        r = shifted(dom, i, 1)
        outbox[i, 0] = blocks[jnp.maximum(pick[0, r], 0)]
        outbox[i, 1] = blocks[jnp.maximum(pick[1, r], 0)]

    arrive()

    def main(i):
        return pltpu.make_async_remote_copy(
            src_ref=outbox.at[i], dst_ref=table.at[pl.ds(NB + 2 * dom, 2), half(rep)], send_sem=send_sem.at[i],
            recv_sem=recv_sem.at[i], device_id=(shifted(dom, i, 1), rep), device_id_type=MESH)

    def passed(i, k):
        part = table.at[pl.ds(NB + 2 * shifted(dom, i, -1), 2), half(k)]
        return pltpu.make_async_remote_copy(
            src_ref=part, dst_ref=part, send_sem=fsend_sem.at[i], recv_sem=frecv_sem.at[i],
            device_id=(dom, sib), device_id_type=MESH)

    @pl.loop(1, DOM)
    def _(step):
        main(shift_of(step)).start()

    @pl.loop(0, NB)
    def _(b):
        table[b, half(rep)] = blocks[b]

    def own(k):
        part = table.at[pl.ds(0, NB), half(k)]
        return pltpu.make_async_remote_copy(src_ref=part, dst_ref=part, send_sem=side_send, recv_sem=side_recv,
                                            device_id=(dom, sib), device_id_type=MESH)

    own(rep).start()

    @pl.loop(1, DOM)
    def _(step):
        i = shift_of(step)
        pltpu.make_async_remote_copy(
            src_ref=outbox.at[i], dst_ref=table.at[pl.ds(NB + 2 * shifted(dom, i, -1), 2), half(rep)],
            send_sem=send_sem.at[i], recv_sem=recv_sem.at[i], device_id=(dom, sib), device_id_type=MESH).wait_recv()
        passed(i, rep).start()

    @pl.loop(1, DOM)
    def _(i):
        main(i).wait_send()
        passed(i, rep).wait_send()
        passed(i, sib).wait_recv()

    own(rep).wait_send()
    own(sib).wait_recv()


def exchange_features(pick, feat):
    return pl.pallas_call(
        feature_kernel,
        out_shape=jax.ShapeDtypeStruct((ENTRIES, BLK, BLK), BF16),
        in_specs=[SM, VM],
        out_specs=VM,
        scratch_shapes=[
            pltpu.VMEM((NB, 64, BLK), BF16),
            pltpu.VMEM((DOM, 2, 64, BLK), BF16),
        ] + [pltpu.SemaphoreType.DMA((DOM,))] * 4 + [pltpu.SemaphoreType.DMA(())] * 2,
        cost_estimate=COST,
        compiler_params=pltpu.CompilerParams(collective_id=0, has_side_effects=True, vmem_limit_bytes=12 << 20),
    )(pick, feat)


def build_list(src, dst, first, lists):
    def step(t, count):
        d = dst[t] - first
        lists[0, count] = t
        lists[1, count] = src[t]
        lists[2, count] = d
        return count + jnp.where((d >= 0) & (d < HALF), 1, 0)

    count = lax.fori_loop(NB, NT, step, 0)
    for u in range(UNROLL):
        lists[0, count + u] = 0
        lists[1, count + u] = 0
        lists[2, count + u] = HALF
    return (count + UNROLL - 1) // UNROLL


def sum_first(first, tiles, table, acc, dims):
    @pl.loop(0, HALF // UNROLL)
    def _(g):
        for u in range(UNROLL):
            b = g * UNROLL + u
            acc[b] = dot(tiles[first + b], table[first + b], dims)


def sum_rest(groups, lists, tiles, table, acc, dims):
    @pl.loop(0, groups)
    def _(g):
        for u in range(UNROLL):
            n = g * UNROLL + u
            acc[lists[2, n]] += dot(tiles[lists[0, n]], table[lists[1, n]], dims)


def first_kernel(src_in, dst_in, tiles, table, mixed, src, dst, acc, lists, load_sem):
    first = pl.multiple_of(lax.axis_index("rep") * HALF, HALF)
    pairs = [(src_in, src), (dst_in, dst)]
    loads = [pltpu.make_async_copy(a, b, load_sem.at[n]) for n, (a, b) in enumerate(pairs)]
    for load in loads:
        load.start()
    sum_first(first, tiles, table, acc, NTR)
    for load in loads:
        load.wait()
    groups = build_list(src, dst, first, lists)
    sum_rest(groups, lists, tiles, table, acc, NTR)

    @pl.loop(0, HALF // UNROLL)
    def _(g):
        at = pl.ds(g * UNROLL, UNROLL)
        mixed[at] = acc[at].astype(BF16)


def first_aggregate(src, dst, tiles, table):
    return pl.pallas_call(
        first_kernel,
        out_shape=jax.ShapeDtypeStruct((HALF, BLK, BLK), BF16),
        in_specs=[ANY, ANY, VM, VM],
        out_specs=VM,
        scratch_shapes=[
            pltpu.SMEM((NT,), jnp.int32),
            pltpu.SMEM((NT,), jnp.int32),
            pltpu.VMEM((HALF + 1, BLK, BLK), F32),
            pltpu.SMEM((3, LIST), jnp.int32),
            pltpu.SemaphoreType.DMA((2,)),
        ],
        cost_estimate=COST,
        compiler_params=pltpu.CompilerParams(vmem_limit_bytes=14 << 20),
    )(src, dst, tiles, table)


def mixed_kernel(pick, mixed, w1, w2, table, hidden, w2_all, own, outbox, w1_all, wbox, wgot,
                 send_sem, recv_sem, fsend_sem, frecv_sem, side_send, side_recv):
    dom, rep = lax.axis_index("dom"), lax.axis_index("rep")
    sib = 1 - rep
    arrive = meet_all(dom, rep)

    @pl.loop(0, HALF)
    def _(b):
        own[rep * HALF + b] = mixed[b]

    wbox[0] = w1[...]
    wbox[1] = jnp.concatenate([w2[...].astype(F32), jnp.zeros((BLK - CLS, BLK), F32)], axis=0).astype(BF16)
    arrive()
    ends = [(mixed, own.at[pl.ds(rep * HALF, HALF)]), (wbox, wgot)]
    side = [
        pltpu.make_async_remote_copy(src_ref=a, dst_ref=b, send_sem=side_send.at[n], recv_sem=side_recv.at[n],
                                     device_id=(dom, sib), device_id_type=MESH)
        for n, (a, b) in enumerate(ends)
    ]
    for c in side:
        c.start()
    side[0].wait()

    def main(i):
        return pltpu.make_async_remote_copy(
            src_ref=outbox.at[i], dst_ref=table.at[NB + 2 * dom + rep], send_sem=send_sem.at[i],
            recv_sem=recv_sem.at[i], device_id=(shifted(dom, i, 1), rep), device_id_type=MESH)

    def pass_on(i):
        e = NB + 2 * shifted(dom, i, -1) + rep
        return pltpu.make_async_remote_copy(
            src_ref=table.at[e], dst_ref=table.at[e], send_sem=fsend_sem.at[i], recv_sem=frecv_sem.at[i],
            device_id=(dom, sib), device_id_type=MESH)

    def taken(i):
        e = NB + 2 * shifted(dom, i, -1) + sib
        return pltpu.make_async_remote_copy(
            src_ref=table.at[e], dst_ref=table.at[e], send_sem=fsend_sem.at[i], recv_sem=frecv_sem.at[i],
            device_id=(dom, sib), device_id_type=MESH)

    @pl.loop(1, DOM)
    def _(step):
        i = shift_of(step)
        outbox[i] = own[jnp.maximum(pick[rep, shifted(dom, i, 1)], 0)]
        main(i).start()

    side[1].wait()
    w1_all[:, :BLK] = wbox[0]
    w1_all[:, BLK:] = wgot[0]
    w2_all[:, :BLK] = wbox[1][:CPAD]
    w2_all[:, BLK:] = wgot[1][:CPAD]

    def activate(e, rows):
        hidden[e] = jnp.maximum(dot(rows, w1_all[...], NN), 0.0).astype(BF16)

    @pl.loop(0, NB // UNROLL)
    def _(g):
        for u in range(UNROLL):
            b = g * UNROLL + u
            rows = own[b]
            table[b] = rows
            activate(b, rows)

    def entry(i, k):
        return NB + 2 * shifted(dom, i, -1) + k

    def take(g):
        for u in range(BATCH):
            i = shift_of(g * BATCH + u + 1)
            main(i).wait_recv()
            pass_on(i).start()

    def take_passed(g):
        for u in range(BATCH):
            taken(shift_of(g * BATCH + u + 1)).wait_recv()

    def activate_batch(g, k):
        for u in range(BATCH):
            e = entry(shift_of(g * BATCH + u + 1), k)
            activate(e, table[e])

    take(0)
    activate_batch(0, rep)

    @pl.loop(1, (DOM - 1) // BATCH)
    def _(g):
        take(g)
        take_passed(g - 1)
        activate_batch(g, rep)
        activate_batch(g - 1, sib)

    take_passed((DOM - 1) // BATCH - 1)
    activate_batch((DOM - 1) // BATCH - 1, sib)

    @pl.loop(1, DOM)
    def _(i):
        main(i).wait_send()
        pass_on(i).wait_send()


def exchange_mixed(pick, mixed, w1, w2):
    return pl.pallas_call(
        mixed_kernel,
        out_shape=(
            jax.ShapeDtypeStruct((ENTRIES, BLK, BLK), BF16),
            jax.ShapeDtypeStruct((ENTRIES, BLK, 2 * BLK), BF16),
            jax.ShapeDtypeStruct((CPAD, 2 * BLK), BF16),
        ),
        in_specs=[SM, VM, VM, VM],
        out_specs=(VM, VM, VM),
        scratch_shapes=[
            pltpu.VMEM((NB, BLK, BLK), BF16),
            pltpu.VMEM((DOM, BLK, BLK), BF16),
            pltpu.VMEM((BLK, 2 * BLK), BF16),
            pltpu.VMEM((2, BLK, BLK), BF16),
            pltpu.VMEM((2, BLK, BLK), BF16),
        ] + [pltpu.SemaphoreType.DMA((DOM,))] * 4 + [pltpu.SemaphoreType.DMA((2,))] * 2,
        cost_estimate=COST,
        compiler_params=pltpu.CompilerParams(collective_id=1, has_side_effects=True, vmem_limit_bytes=12 << 20),
    )(pick, mixed, w1, w2)


def second_kernel(scale, src_in, dst_in, labels, tiles, table, hidden, w2, pay, hidden_out, src, dst, acc, grad, lists, sem,
                  load_sem):
    first = lax.axis_index("rep") * HALF
    loads = [pltpu.make_async_copy(a, b, load_sem.at[n]) for n, (a, b) in enumerate([(src_in, src), (dst_in, dst)])]
    for load in loads:
        load.start()
    out = pltpu.make_async_copy(hidden.at[pl.ds(0, NB), :, pl.ds(0, BLK)], hidden_out, sem)
    out.start()
    sum_first(first, tiles, hidden, acc, NN)
    for load in loads:
        load.wait()
    groups = build_list(src, dst, first, lists)
    sum_rest(groups, lists, tiles, hidden, acc, NN)
    pay[...] = jnp.zeros_like(pay)
    grad[HALF] = jnp.zeros((BLK, 2 * BLK), BF16)
    w2_t = w2[...]
    kinds = lax.broadcasted_iota(jnp.int32, (CPAD, ROWS), 0)

    def classify(g, loss):
        at = pl.ds(g * WIDE, WIDE)
        second = acc[at].reshape(ROWS, 2 * BLK).astype(BF16)
        logits = dot(w2_t, second, NTR)
        powers = jnp.where(kinds < CLS, jnp.exp(logits), 0.0)
        total = jnp.sum(powers, axis=0, keepdims=True)
        hot = kinds == labels[lax.axis_index("rep") * (HALF // WIDE) + g]
        loss = loss + jnp.log(total) - jnp.sum(jnp.where(hot, logits, 0.0), axis=0, keepdims=True)
        grad_logits = ((powers * (1.0 / total) - jnp.where(hot, 1.0, 0.0)) * scale).astype(BF16)
        pay[BLK:BLK + CPAD] += dot(grad_logits, second, NN)
        grad[at] = dot(grad_logits, w2_t, TN).astype(BF16).reshape(WIDE, BLK, 2 * BLK)
        return loss

    loss = lax.fori_loop(0, HALF // WIDE, classify, jnp.zeros((1, ROWS), F32))
    pay[BLK + CPAD:] = jnp.zeros((PAY - BLK - CPAD, 2 * BLK), F32) + jnp.sum(loss)

    def back(t, e, d):
        part = dot(tiles[t], grad[d], TN)
        return jnp.where(hidden[e] > 0, part, 0.0).astype(BF16)

    def pair(a, b):
        rows = jnp.concatenate([table[a[1]], table[b[1]]], axis=0)
        return dot(rows, jnp.concatenate([back(*a), back(*b)], axis=0), TN)

    def add_pairs(at):
        total = pair(at[0], at[1])
        for u in range(2, UNROLL, 2):
            total = total + pair(at[u], at[u + 1])
        pay[:BLK] += total

    @pl.loop(0, HALF // UNROLL)
    def _(g):
        at = [g * UNROLL + u for u in range(UNROLL)]
        add_pairs([(first + b, first + b, b) for b in at])

    @pl.loop(0, groups)
    def _(g):
        at = [g * UNROLL + u for u in range(UNROLL)]
        add_pairs([(lists[0, n], lists[1, n], lists[2, n]) for n in at])

    out.wait()


def second_layer(scale, src, dst, labels, tiles, table, hidden, w2):
    return pl.pallas_call(
        functools.partial(second_kernel, scale),
        out_shape=(
            jax.ShapeDtypeStruct((PAY, 2 * BLK), F32),
            jax.ShapeDtypeStruct((NB, BLK, BLK), BF16),
        ),
        in_specs=[ANY, ANY, VM, VM, VM, VM, VM],
        out_specs=(VM, ANY),
        scratch_shapes=[
            pltpu.SMEM((NT,), jnp.int32),
            pltpu.SMEM((NT,), jnp.int32),
            pltpu.VMEM((HALF + 1, BLK, 2 * BLK), F32),
            pltpu.VMEM((HALF + 1, BLK, 2 * BLK), BF16),
            pltpu.SMEM((3, LIST), jnp.int32),
            pltpu.SemaphoreType.DMA(()),
            pltpu.SemaphoreType.DMA((2,)),
        ],
        cost_estimate=COST,
        compiler_params=pltpu.CompilerParams(vmem_limit_bytes=12 << 20),
    )(src, dst, labels, tiles, table, hidden, w2)


def sum_kernel(pay, out, got, mine, parts, plane, psum, send_sem, recv_sem):
    dom, rep = lax.axis_index("dom"), lax.axis_index("rep")
    x, z, y = coords(dom)
    zy = z * 4 + y
    sib = 1 - rep

    def along_x(j):
        return ((x + j) % 4) * 16 + zy, (x + j) % 4

    def in_plane(j):
        return x * 16 + ((z + j // 4) % 4) * 4 + (y + j % 4) % 4

    barrier = pltpu.get_barrier_semaphore()
    pl.semaphore_signal(barrier, inc=1, device_id=(dom, sib), device_id_type=MESH)
    for j in range(1, 4):
        pl.semaphore_signal(barrier, inc=1, device_id=(along_x(j)[0], rep), device_id_type=MESH)
    for j in range(1, 16):
        pl.semaphore_signal(barrier, inc=1, device_id=(in_plane(j), rep), device_id_type=MESH)
    pl.semaphore_wait(barrier, 19)

    def copy(a, b, n, to):
        return pltpu.make_async_remote_copy(src_ref=a, dst_ref=b, send_sem=send_sem.at[n], recv_sem=recv_sem.at[n],
                                            device_id=to, device_id_type=MESH)

    side = copy(pay.at[:, pl.ds(BLK, BLK)], got, 0, (dom, sib))
    side.start()
    side.wait()
    mine[...] = pay[:, :BLK] + got[...]

    cut = []
    for j in range(1, 4):
        to, tx = along_x(j)
        cut.append(copy(mine.at[pl.ds(pl.multiple_of(tx * PART, 8), PART)], parts.at[j], j, (to, rep)))
        cut[-1].start()
    total = mine[pl.ds(pl.multiple_of(x * PART, 8), PART)]
    for j in range(1, 4):
        cut[j - 1].wait()
        total = total + parts[j]
    psum[...] = total

    across = []
    for j in range(1, 16):
        across.append(copy(psum, plane.at[j], 3 + j, (in_plane(j), rep)))
        across[-1].start()
    for j in range(1, 16):
        across[j - 1].wait()
    plane[0] = psum[...]
    total = plane[0]
    for j in range(1, 16):
        total = total + plane[j]
    here = pl.ds(pl.multiple_of(x * PART, 8), PART)
    out[here] = total

    back = []
    for j in range(1, 4):
        back.append(copy(out.at[here], out.at[here], 18 + j, (along_x(j)[0], rep)))
        back[-1].start()
    for c in back:
        c.wait_send()
    for j in range(1, 4):
        there = pl.ds(pl.multiple_of(((x + 4 - j) % 4) * PART, 8), PART)
        copy(out.at[there], out.at[there], 18 + j, (along_x(j)[0], rep)).wait_recv()


def sum_all(pay):
    return pl.pallas_call(
        sum_kernel,
        out_shape=jax.ShapeDtypeStruct((PAY, BLK), F32),
        in_specs=[VM],
        out_specs=VM,
        scratch_shapes=[
            pltpu.VMEM((PAY, BLK), F32),
            pltpu.VMEM((PAY, BLK), F32),
            pltpu.VMEM((4, PART, BLK), F32),
            pltpu.VMEM((16, PART, BLK), F32),
            pltpu.VMEM((PART, BLK), F32),
            pltpu.SemaphoreType.DMA((22,)),
            pltpu.SemaphoreType.DMA((22,)),
        ],
        cost_estimate=COST,
        compiler_params=pltpu.CompilerParams(collective_id=2, has_side_effects=True, vmem_limit_bytes=8 << 20),
    )(pay)


def per_device(features, weight_first, weight_second, labels, send_index, tile_src, tile_dst, tile_values):
    node_count = lax.axis_size("dom") * NB * BLK
    pick = send_index[0].T
    table = exchange_features(pick, features.T)
    mixed = first_aggregate(tile_src, tile_dst, tile_values, table)
    mixed_table, hidden, w2 = exchange_mixed(pick, mixed, weight_first, weight_second.T)
    pay, hidden_out = second_layer(
        1.0 / node_count**0.5, tile_src, tile_dst, labels.reshape(NB // WIDE, 1, ROWS), tile_values, mixed_table,
        hidden, w2)
    total = sum_all(pay)
    grad_first = total[:BLK]
    grad_second = total[BLK:BLK + CLS].T
    loss = total[BLK + CPAD, 0] / node_count
    return hidden_out.reshape(NB * BLK, BLK), grad_first, grad_second, loss


def solution(mesh):
    return jax.shard_map(
        per_device,
        mesh=mesh,
        in_specs=(P("dom", "rep"), P(None, "rep"), P("rep", None), P("dom"), P("dom", None, None), P("dom"), P("dom"),
                  P("dom", None, None)),
        out_specs=(P("dom", "rep"), P(None, "rep"), P("rep", None), P()),
        check_vma=False,
    )
```

```python
import functools

import jax
import jax.numpy as jnp
from jax import lax
from jax.experimental import pallas as pl
from jax.experimental.pallas import tpu as pltpu
from jax.sharding import PartitionSpec as P

MESH = pl.DeviceIdType.MESH
BLK = 128
NB = 64
HALF = NB // 2
S = 2
DOM = 64
NT = 256
ENTRIES = NB + DOM * S
CLS = 47
CPAD = 48
UNROLL = 16
BATCH = 3
LAG = 4
WIDE = 8
ROWS = WIDE * BLK
LIST = NT + UNROLL
PAY = 192
PART = PAY // 4
F32 = jnp.float32
BF16 = jnp.bfloat16

VM = pl.BlockSpec(memory_space=pltpu.VMEM)
SM = pl.BlockSpec(memory_space=pltpu.SMEM)
ANY = pl.BlockSpec(memory_space=pl.ANY)
COST = pl.CostEstimate(flops=10**10, bytes_accessed=10**8, transcendentals=0)


def coords(dom):
    return lax.div(dom, 16), lax.rem(lax.div(dom, 4), 4), lax.rem(dom, 4)


def shifted(dom, i, sign):
    x, z, y = coords(dom)
    dx, dz, dy = coords(i)
    return (lax.rem(x + sign * dx + 4, 4) * 16 + lax.rem(z + sign * dz + 4, 4) * 4 + lax.rem(y + sign * dy + 4, 4))


def shift_of(step):
    return lax.rem(step * 10, 63) + 1


def meet_all(dom, rep):
    barrier = pltpu.get_barrier_semaphore()
    pl.semaphore_signal(barrier, inc=1, device_id=(dom, 1 - rep), device_id_type=MESH)
    x, z, y = coords(dom)
    xs = [lax.rem(x + d, 4) * 16 for d in range(4)]
    zs = [lax.rem(z + d, 4) * 4 for d in range(4)]
    ys = [lax.rem(y + d, 4) for d in range(4)]
    for i in range(1, DOM):
        peer = xs[i // 16] + zs[i // 4 % 4] + ys[i % 4]
        pl.semaphore_signal(barrier, inc=1, device_id=(peer, rep), device_id_type=MESH)
    return lambda: pl.semaphore_wait(barrier, DOM)


def dot(a, b, dims):
    return lax.dot_general(a, b, (dims, ((), ())), preferred_element_type=F32)


NN = ((1,), (0,))
TN = ((0,), (0,))
NTR = ((1,), (1,))


def feature_kernel(pick, feat, table, blocks, outbox, send_sem, recv_sem, fsend_sem, frecv_sem, side_send, side_recv):
    dom, rep = lax.axis_index("dom"), lax.axis_index("rep")
    sib = 1 - rep
    arrive = meet_all(dom, rep)

    def half(k):
        return pl.ds(pl.multiple_of(k * 64, 64), 64)

    @pl.loop(0, NB)
    def _(b):
        blocks[b] = feat[:, pl.ds(pl.multiple_of(b * BLK, BLK), BLK)]

    @pl.loop(1, DOM)
    def _(step):
        i = shift_of(step)
        r = shifted(dom, i, 1)
        outbox[i, 0] = blocks[jnp.maximum(pick[0, r], 0)]
        outbox[i, 1] = blocks[jnp.maximum(pick[1, r], 0)]

    arrive()

    def main(i):
        return pltpu.make_async_remote_copy(
            src_ref=outbox.at[i], dst_ref=table.at[pl.ds(NB + 2 * dom, 2), half(rep)], send_sem=send_sem.at[i],
            recv_sem=recv_sem.at[i], device_id=(shifted(dom, i, 1), rep), device_id_type=MESH)

    def passed(i, k):
        part = table.at[pl.ds(NB + 2 * shifted(dom, i, -1), 2), half(k)]
        return pltpu.make_async_remote_copy(
            src_ref=part, dst_ref=part, send_sem=fsend_sem.at[i], recv_sem=frecv_sem.at[i],
            device_id=(dom, sib), device_id_type=MESH)

    @pl.loop(1, DOM)
    def _(step):
        main(shift_of(step)).start()

    @pl.loop(0, NB)
    def _(b):
        table[b, half(rep)] = blocks[b]

    def own(k):
        part = table.at[pl.ds(0, NB), half(k)]
        return pltpu.make_async_remote_copy(src_ref=part, dst_ref=part, send_sem=side_send, recv_sem=side_recv,
                                            device_id=(dom, sib), device_id_type=MESH)

    own(rep).start()

    def take(step):
        i = shift_of(step)
        pltpu.make_async_remote_copy(
            src_ref=outbox.at[i], dst_ref=table.at[pl.ds(NB + 2 * shifted(dom, i, -1), 2), half(rep)],
            send_sem=send_sem.at[i], recv_sem=recv_sem.at[i], device_id=(dom, sib), device_id_type=MESH).wait_recv()
        passed(i, rep).start()
        main(i).wait_send()

    def finish(step):
        i = shift_of(step)
        passed(i, rep).wait_send()
        passed(i, sib).wait_recv()

    @pl.loop(1, 1 + LAG)
    def _(step):
        take(step)

    @pl.loop(1 + LAG, DOM)
    def _(step):
        take(step)
        finish(step - LAG)

    @pl.loop(DOM - LAG, DOM)
    def _(step):
        finish(step)

    own(rep).wait_send()
    own(sib).wait_recv()


def exchange_features(pick, feat):
    return pl.pallas_call(
        feature_kernel,
        out_shape=jax.ShapeDtypeStruct((ENTRIES, BLK, BLK), BF16),
        in_specs=[SM, VM],
        out_specs=VM,
        scratch_shapes=[
            pltpu.VMEM((NB, 64, BLK), BF16),
            pltpu.VMEM((DOM, 2, 64, BLK), BF16),
        ] + [pltpu.SemaphoreType.DMA((DOM,))] * 4 + [pltpu.SemaphoreType.DMA(())] * 2,
        cost_estimate=COST,
        compiler_params=pltpu.CompilerParams(collective_id=0, has_side_effects=True, vmem_limit_bytes=12 << 20),
    )(pick, feat)


def build_list(src, dst, first, lists):
    def step(t, count):
        d = dst[t] - first
        lists[0, count] = t
        lists[1, count] = src[t]
        lists[2, count] = d
        return count + jnp.where((d >= 0) & (d < HALF), 1, 0)

    count = lax.fori_loop(NB, NT, step, 0, unroll=8)
    for u in range(UNROLL):
        lists[0, count + u] = 0
        lists[1, count + u] = 0
        lists[2, count + u] = HALF
    return (count + UNROLL - 1) // UNROLL


def sum_first(first, tiles, table, acc, dims):
    @pl.loop(0, HALF // UNROLL)
    def _(g):
        for u in range(UNROLL):
            b = g * UNROLL + u
            acc[b] = dot(tiles[first + b], table[first + b], dims)


def sum_rest(groups, lists, tiles, table, acc, dims):
    @pl.loop(0, groups)
    def _(g):
        for u in range(UNROLL):
            n = g * UNROLL + u
            acc[lists[2, n]] += dot(tiles[lists[0, n]], table[lists[1, n]], dims)


def first_kernel(src_in, dst_in, tiles, table, mixed, src, dst, acc, lists, load_sem):
    first = pl.multiple_of(lax.axis_index("rep") * HALF, HALF)
    pairs = [(src_in, src), (dst_in, dst)]
    loads = [pltpu.make_async_copy(a, b, load_sem.at[n]) for n, (a, b) in enumerate(pairs)]
    for load in loads:
        load.start()
    sum_first(first, tiles, table, acc, NTR)
    for load in loads:
        load.wait()
    groups = build_list(src, dst, first, lists)
    sum_rest(groups, lists, tiles, table, acc, NTR)

    @pl.loop(0, HALF // UNROLL)
    def _(g):
        at = pl.ds(g * UNROLL, UNROLL)
        mixed[at] = acc[at].astype(BF16)


def first_aggregate(src, dst, tiles, table):
    return pl.pallas_call(
        first_kernel,
        out_shape=jax.ShapeDtypeStruct((HALF, BLK, BLK), BF16),
        in_specs=[ANY, ANY, VM, VM],
        out_specs=VM,
        scratch_shapes=[
            pltpu.SMEM((NT,), jnp.int32),
            pltpu.SMEM((NT,), jnp.int32),
            pltpu.VMEM((HALF + 1, BLK, BLK), F32),
            pltpu.SMEM((3, LIST), jnp.int32),
            pltpu.SemaphoreType.DMA((2,)),
        ],
        cost_estimate=COST,
        compiler_params=pltpu.CompilerParams(vmem_limit_bytes=14 << 20),
    )(src, dst, tiles, table)


def mixed_kernel(pick, mixed, w1, w2, table, hidden, w2_all, own, outbox, w1_all, wbox, wgot,
                 send_sem, recv_sem, fsend_sem, frecv_sem, side_send, side_recv):
    dom, rep = lax.axis_index("dom"), lax.axis_index("rep")
    sib = 1 - rep
    arrive = meet_all(dom, rep)

    @pl.loop(0, HALF)
    def _(b):
        own[rep * HALF + b] = mixed[b]

    wbox[0] = w1[...]
    wbox[1] = jnp.concatenate([w2[...].astype(F32), jnp.zeros((BLK - CLS, BLK), F32)], axis=0).astype(BF16)
    arrive()
    ends = [(mixed, own.at[pl.ds(rep * HALF, HALF)]), (wbox, wgot)]
    side = [
        pltpu.make_async_remote_copy(src_ref=a, dst_ref=b, send_sem=side_send.at[n], recv_sem=side_recv.at[n],
                                     device_id=(dom, sib), device_id_type=MESH)
        for n, (a, b) in enumerate(ends)
    ]
    for c in side:
        c.start()
    side[0].wait()

    def main(i):
        return pltpu.make_async_remote_copy(
            src_ref=outbox.at[i], dst_ref=table.at[NB + 2 * dom + rep], send_sem=send_sem.at[i],
            recv_sem=recv_sem.at[i], device_id=(shifted(dom, i, 1), rep), device_id_type=MESH)

    def pass_on(i):
        e = NB + 2 * shifted(dom, i, -1) + rep
        return pltpu.make_async_remote_copy(
            src_ref=table.at[e], dst_ref=table.at[e], send_sem=fsend_sem.at[i], recv_sem=frecv_sem.at[i],
            device_id=(dom, sib), device_id_type=MESH)

    def taken(i):
        e = NB + 2 * shifted(dom, i, -1) + sib
        return pltpu.make_async_remote_copy(
            src_ref=table.at[e], dst_ref=table.at[e], send_sem=fsend_sem.at[i], recv_sem=frecv_sem.at[i],
            device_id=(dom, sib), device_id_type=MESH)

    @pl.loop(1, DOM)
    def _(step):
        i = shift_of(step)
        outbox[i] = own[jnp.maximum(pick[rep, shifted(dom, i, 1)], 0)]
        main(i).start()

    side[1].wait()
    w1_all[:, :BLK] = wbox[0]
    w1_all[:, BLK:] = wgot[0]
    w2_all[:, :BLK] = wbox[1][:CPAD]
    w2_all[:, BLK:] = wgot[1][:CPAD]

    def activate(e, rows):
        hidden[e] = jnp.maximum(dot(rows, w1_all[...], NN), 0.0).astype(BF16)

    @pl.loop(0, NB // UNROLL)
    def _(g):
        for u in range(UNROLL):
            b = g * UNROLL + u
            rows = own[b]
            table[b] = rows
            activate(b, rows)

    def entry(i, k):
        return NB + 2 * shifted(dom, i, -1) + k

    def take(g):
        for u in range(BATCH):
            i = shift_of(g * BATCH + u + 1)
            main(i).wait_recv()
            pass_on(i).start()

    def take_passed(g):
        for u in range(BATCH):
            i = shift_of(g * BATCH + u + 1)
            taken(i).wait_recv()
            main(i).wait_send()
            pass_on(i).wait_send()

    def activate_batch(g, k):
        for u in range(BATCH):
            e = entry(shift_of(g * BATCH + u + 1), k)
            activate(e, table[e])

    take(0)
    activate_batch(0, rep)

    @pl.loop(1, (DOM - 1) // BATCH)
    def _(g):
        take(g)
        take_passed(g - 1)
        activate_batch(g, rep)
        activate_batch(g - 1, sib)

    take_passed((DOM - 1) // BATCH - 1)
    activate_batch((DOM - 1) // BATCH - 1, sib)


def exchange_mixed(pick, mixed, w1, w2):
    return pl.pallas_call(
        mixed_kernel,
        out_shape=(
            jax.ShapeDtypeStruct((ENTRIES, BLK, BLK), BF16),
            jax.ShapeDtypeStruct((ENTRIES, BLK, 2 * BLK), BF16),
            jax.ShapeDtypeStruct((CPAD, 2 * BLK), BF16),
        ),
        in_specs=[SM, VM, VM, VM],
        out_specs=(VM, VM, VM),
        scratch_shapes=[
            pltpu.VMEM((NB, BLK, BLK), BF16),
            pltpu.VMEM((DOM, BLK, BLK), BF16),
            pltpu.VMEM((BLK, 2 * BLK), BF16),
            pltpu.VMEM((2, BLK, BLK), BF16),
            pltpu.VMEM((2, BLK, BLK), BF16),
        ] + [pltpu.SemaphoreType.DMA((DOM,))] * 4 + [pltpu.SemaphoreType.DMA((2,))] * 2,
        cost_estimate=COST,
        compiler_params=pltpu.CompilerParams(collective_id=1, has_side_effects=True, vmem_limit_bytes=12 << 20),
    )(pick, mixed, w1, w2)


def second_kernel(scale, src_in, dst_in, labels, tiles, table, hidden, w2, pay, hidden_out, src, dst, acc, grad, lists, sem,
                  load_sem):
    first = lax.axis_index("rep") * HALF
    loads = [pltpu.make_async_copy(a, b, load_sem.at[n]) for n, (a, b) in enumerate([(src_in, src), (dst_in, dst)])]
    for load in loads:
        load.start()
    out = pltpu.make_async_copy(hidden.at[pl.ds(0, NB), :, pl.ds(0, BLK)], hidden_out, sem)
    out.start()
    sum_first(first, tiles, hidden, acc, NN)
    for load in loads:
        load.wait()
    groups = build_list(src, dst, first, lists)
    sum_rest(groups, lists, tiles, hidden, acc, NN)
    pay[...] = jnp.zeros_like(pay)
    grad[HALF] = jnp.zeros((BLK, 2 * BLK), BF16)
    w2_t = w2[...]
    kinds = lax.broadcasted_iota(jnp.int32, (CPAD, ROWS), 0)

    def classify(g, loss):
        at = pl.ds(g * WIDE, WIDE)
        second = acc[at].reshape(ROWS, 2 * BLK).astype(BF16)
        logits = dot(w2_t, second, NTR)
        powers = jnp.where(kinds < CLS, jnp.exp(logits), 0.0)
        total = jnp.sum(powers, axis=0, keepdims=True)
        hot = kinds == labels[lax.axis_index("rep") * (HALF // WIDE) + g]
        loss = loss + jnp.log(total) - jnp.sum(jnp.where(hot, logits, 0.0), axis=0, keepdims=True)
        grad_logits = ((powers * (1.0 / total) - jnp.where(hot, 1.0, 0.0)) * scale).astype(BF16)
        pay[BLK:BLK + CPAD] += dot(grad_logits, second, NN)
        grad[at] = dot(grad_logits, w2_t, TN).astype(BF16).reshape(WIDE, BLK, 2 * BLK)
        return loss

    loss = lax.fori_loop(0, HALF // WIDE, classify, jnp.zeros((1, ROWS), F32))
    pay[BLK + CPAD:] = jnp.zeros((PAY - BLK - CPAD, 2 * BLK), F32) + jnp.sum(loss)

    def back(t, e, d):
        part = dot(tiles[t], grad[d], TN).astype(BF16)
        return jnp.where(hidden[e] > 0, part, jnp.zeros_like(part))

    def add_all(at):
        masked = jnp.concatenate([back(*each) for each in at], axis=0)
        rows = jnp.concatenate([table[each[1]] for each in at], axis=0)
        pay[:BLK] += dot(rows, masked, TN)

    @pl.loop(0, HALF // UNROLL)
    def _(g):
        at = [g * UNROLL + u for u in range(UNROLL)]
        add_all([(first + b, first + b, b) for b in at])

    @pl.loop(0, groups)
    def _(g):
        at = [g * UNROLL + u for u in range(UNROLL)]
        add_all([(lists[0, n], lists[1, n], lists[2, n]) for n in at])

    out.wait()


def second_layer(scale, src, dst, labels, tiles, table, hidden, w2):
    return pl.pallas_call(
        functools.partial(second_kernel, scale),
        out_shape=(
            jax.ShapeDtypeStruct((PAY, 2 * BLK), F32),
            jax.ShapeDtypeStruct((NB, BLK, BLK), BF16),
        ),
        in_specs=[ANY, ANY, VM, VM, VM, VM, VM],
        out_specs=(VM, ANY),
        scratch_shapes=[
            pltpu.SMEM((NT,), jnp.int32),
            pltpu.SMEM((NT,), jnp.int32),
            pltpu.VMEM((HALF + 1, BLK, 2 * BLK), F32),
            pltpu.VMEM((HALF + 1, BLK, 2 * BLK), BF16),
            pltpu.SMEM((3, LIST), jnp.int32),
            pltpu.SemaphoreType.DMA(()),
            pltpu.SemaphoreType.DMA((2,)),
        ],
        cost_estimate=COST,
        compiler_params=pltpu.CompilerParams(vmem_limit_bytes=12 << 20),
    )(src, dst, labels, tiles, table, hidden, w2)


def sum_kernel(pay, out, parts, zs, ys, first, second, send_sem, recv_sem):
    dom, rep = lax.axis_index("dom"), lax.axis_index("rep")
    x, z, y = coords(dom)
    sib = 1 - rep
    cores = (rep, sib)

    def along_x(j):
        return lax.rem(x + j, 4)

    def x_peer(j):
        return along_x(j) * 16 + z * 4 + y

    def z_peer(j):
        return x * 16 + lax.rem(z + j, 4) * 4 + y

    def y_peer(j):
        return x * 16 + z * 4 + lax.rem(y + j, 4)

    barrier = pltpu.get_barrier_semaphore()
    peers = [(dom, sib)] + [(x_peer(j), c) for j in range(1, 4) for c in cores]
    peers += [(f(j), rep) for j in range(1, 4) for f in (z_peer, y_peer)]
    for peer in peers:
        pl.semaphore_signal(barrier, inc=1, device_id=peer, device_id_type=MESH)
    pl.semaphore_wait(barrier, len(peers))

    def copy(a, b, n, to):
        return pltpu.make_async_remote_copy(src_ref=a, dst_ref=b, send_sem=send_sem.at[n], recv_sem=recv_sem.at[n],
                                            device_id=to, device_id_type=MESH)

    def rows(k):
        return pl.ds(pl.multiple_of(k * PART, 8), PART)

    cut = []
    for j in (2, 1, 3, 0):
        for k in (1, 0):
            if j or k:
                cut.append(copy(pay.at[rows(along_x(j)), pl.ds(k * BLK, BLK)], parts.at[k, j], 4 * k + j,
                                (x_peer(j), cores[k])))
                cut[-1].start()
    total = pay[rows(x), :BLK]
    for c in cut:
        c.wait()
    for j in range(4):
        for k in range(2):
            if j or k:
                total = total + parts[k, j]
    first[...] = total

    def sum_over(mine, got, n, peer):
        sent = [copy(mine, got.at[j], n + j, (peer(j), rep)) for j in (2, 1, 3)]
        for c in sent:
            c.start()
        for c in sent:
            c.wait()
        return mine[...] + got[1] + got[2] + got[3]

    second[...] = sum_over(first, zs, 8, z_peer)
    out[rows(x)] = sum_over(second, ys, 12, y_peer)

    here = out.at[rows(x)]
    back = [copy(here, here, 16 + j, (x_peer(j), rep)) for j in (2, 1, 3)]
    for c in back:
        c.start()
    for j in (2, 1, 3):
        there = out.at[rows(along_x(4 - j))]
        copy(there, there, 16 + j, (x_peer(j), rep)).wait_recv()
    for c in back:
        c.wait_send()


def sum_all(pay):
    return pl.pallas_call(
        sum_kernel,
        out_shape=jax.ShapeDtypeStruct((PAY, BLK), F32),
        in_specs=[VM],
        out_specs=VM,
        scratch_shapes=[
            pltpu.VMEM((2, 4, PART, BLK), F32),
            pltpu.VMEM((4, PART, BLK), F32),
            pltpu.VMEM((4, PART, BLK), F32),
            pltpu.VMEM((PART, BLK), F32),
            pltpu.VMEM((PART, BLK), F32),
            pltpu.SemaphoreType.DMA((20,)),
            pltpu.SemaphoreType.DMA((20,)),
        ],
        cost_estimate=COST,
        compiler_params=pltpu.CompilerParams(collective_id=2, has_side_effects=True, vmem_limit_bytes=8 << 20),
    )(pay)


def per_device(features, weight_first, weight_second, labels, send_index, tile_src, tile_dst, tile_values):
    node_count = lax.axis_size("dom") * NB * BLK
    pick = send_index[0].T
    table = exchange_features(pick, features.T)
    mixed = first_aggregate(tile_src, tile_dst, tile_values, table)
    mixed_table, hidden, w2 = exchange_mixed(pick, mixed, weight_first, weight_second.T)
    pay, hidden_out = second_layer(
        1.0 / node_count**0.5, tile_src, tile_dst, labels.reshape(NB // WIDE, 1, ROWS), tile_values, mixed_table,
        hidden, w2)
    total = sum_all(pay)
    grad_first = total[:BLK]
    grad_second = total[BLK:BLK + CLS].T
    loss = total[BLK + CPAD, 0] / node_count
    return hidden_out.reshape(NB * BLK, BLK), grad_first, grad_second, loss


def solution(mesh):
    return jax.shard_map(
        per_device,
        mesh=mesh,
        in_specs=(P("dom", "rep"), P(None, "rep"), P("rep", None), P("dom"), P("dom", None, None), P("dom"), P("dom"),
                  P("dom", None, None)),
        out_specs=(P("dom", "rep"), P(None, "rep"), P("rep", None), P()),
        check_vma=False,
    )
```

```python
import functools

import jax
import jax.numpy as jnp
from jax import lax
from jax.experimental import pallas as pl
from jax.experimental.pallas import tpu as pltpu
from jax.sharding import PartitionSpec as P

MESH = pl.DeviceIdType.MESH
BLK = 128
NB = 64
HALF = NB // 2
S = 2
DOM = 64
NT = 256
ENTRIES = NB + DOM * S
CLS = 47
CPAD = 48
UNROLL = 16
BATCH = 3
MANY = 32
WIDE = 8
ROWS = WIDE * BLK
LIST = NT + UNROLL
PAY = 192
PART = PAY // 4
F32 = jnp.float32
BF16 = jnp.bfloat16

VM = pl.BlockSpec(memory_space=pltpu.VMEM)
SM = pl.BlockSpec(memory_space=pltpu.SMEM)
ANY = pl.BlockSpec(memory_space=pl.ANY)
COST = pl.CostEstimate(flops=10**10, bytes_accessed=10**8, transcendentals=0)


def coords(dom):
    return lax.div(dom, 16), lax.rem(lax.div(dom, 4), 4), lax.rem(dom, 4)


def shifted(dom, i, sign):
    x, z, y = coords(dom)
    dx, dz, dy = coords(i)
    return (lax.rem(x + sign * dx + 4, 4) * 16 + lax.rem(z + sign * dz + 4, 4) * 4 + lax.rem(y + sign * dy + 4, 4))


def shift_of(step):
    return lax.rem(step * 10, 63) + 1


def hops(i):
    return sum(min(d, 4 - d) for d in (i // 16, i // 4 % 4, i % 4))


def meet_all(dom, rep, sibling):
    barrier = pltpu.get_barrier_semaphore()
    x, z, y = coords(dom)
    xs = [lax.rem(x + d, 4) * 16 for d in range(4)]
    zs = [lax.rem(z + d, 4) * 4 for d in range(4)]
    ys = [lax.rem(y + d, 4) for d in range(4)]
    for i in sorted(range(1, DOM), key=lambda i: -hops(i)):
        peer = xs[i // 16] + zs[i // 4 % 4] + ys[i % 4]
        pl.semaphore_signal(barrier, inc=1, device_id=(peer, rep), device_id_type=MESH)
    if sibling:
        pl.semaphore_signal(barrier, inc=1, device_id=(dom, 1 - rep), device_id_type=MESH)
    return lambda: pl.semaphore_wait(barrier, DOM if sibling else DOM - 1)


def dot(a, b, dims):
    return lax.dot_general(a, b, (dims, ((), ())), preferred_element_type=F32)


NN = ((1,), (0,))
TN = ((0,), (0,))
NTR = ((1,), (1,))


def send_copy(dom, rep, i, outbox, landing, send_sem, recv_sem):
    return pltpu.make_async_remote_copy(
        src_ref=outbox.at[i], dst_ref=landing, send_sem=send_sem.at[i], recv_sem=recv_sem.at[i],
        device_id=(shifted(dom, i, 1), rep), device_id_type=MESH)


def pack(dom, pick, blocks, outbox):
    @pl.loop(1, DOM)
    def _(step):
        i = shift_of(step)
        r = shifted(dom, i, 1)
        outbox[i, 0] = blocks[jnp.maximum(pick[0, r], 0)]
        outbox[i, 1] = blocks[jnp.maximum(pick[1, r], 0)]


def feature_kernel(pick, feat, table, blocks, outbox, send_sem, recv_sem):
    dom, rep = lax.axis_index("dom"), lax.axis_index("rep")
    arrive = meet_all(dom, rep, False)

    @pl.loop(0, NB)
    def _(b):
        blocks[b] = feat[:, pl.ds(pl.multiple_of(b * BLK, BLK), BLK)]

    pack(dom, pick, blocks, outbox)
    arrive()

    def main(i, s):
        return send_copy(dom, rep, i, outbox, table.at[pl.ds(NB + 2 * s, 2)], send_sem, recv_sem)

    @pl.loop(1, DOM)
    def _(step):
        main(shift_of(step), dom).start()

    @pl.loop(0, NB)
    def _(b):
        table[b] = blocks[b]

    @pl.loop(1, DOM)
    def _(step):
        i = shift_of(step)
        main(i, shifted(dom, i, -1)).wait_recv()
        main(i, dom).wait_send()


def exchange_features(pick, feat):
    return pl.pallas_call(
        feature_kernel,
        out_shape=jax.ShapeDtypeStruct((ENTRIES, 64, BLK), BF16),
        in_specs=[SM, VM],
        out_specs=VM,
        scratch_shapes=[
            pltpu.VMEM((NB, 64, BLK), BF16),
            pltpu.VMEM((DOM, 2, 64, BLK), BF16),
        ] + [pltpu.SemaphoreType.DMA((DOM,))] * 2,
        cost_estimate=COST,
        compiler_params=pltpu.CompilerParams(collective_id=0, has_side_effects=True, vmem_limit_bytes=12 << 20),
    )(pick, feat)


def first_kernel(src_in, dst_in, tiles, table, mixed, src, dst, acc, load_sem):
    pairs = [(src_in, src), (dst_in, dst)]
    loads = [pltpu.make_async_copy(a, b, load_sem.at[n]) for n, (a, b) in enumerate(pairs)]
    for load in loads:
        load.start()

    @pl.loop(0, NB // MANY)
    def _(g):
        for u in range(MANY):
            b = g * MANY + u
            acc[b] = dot(table[b], tiles[b], NTR)

    for load in loads:
        load.wait()

    @pl.loop(NB // MANY, NT // MANY)
    def _(g):
        for u in range(MANY):
            t = g * MANY + u
            acc[dst[t]] += dot(table[src[t]], tiles[t], NTR)

    @pl.loop(0, NB // MANY)
    def _(g):
        at = pl.ds(g * MANY, MANY)
        mixed[at] = acc[at].astype(BF16)


def first_aggregate(src, dst, tiles, table):
    return pl.pallas_call(
        first_kernel,
        out_shape=jax.ShapeDtypeStruct((NB, 64, BLK), BF16),
        in_specs=[ANY, ANY, VM, VM],
        out_specs=VM,
        scratch_shapes=[
            pltpu.SMEM((NT,), jnp.int32),
            pltpu.SMEM((NT,), jnp.int32),
            pltpu.VMEM((NB, 64, BLK), F32),
            pltpu.SemaphoreType.DMA((2,)),
        ],
        cost_estimate=COST,
        compiler_params=pltpu.CompilerParams(vmem_limit_bytes=14 << 20),
    )(src, dst, tiles, table)


def mixed_kernel(pick, mixed, w1, w2, table, hidden, w2_all, outbox, w1_all, wbox, wgot,
                 send_sem, recv_sem, fsend_sem, frecv_sem, side_send, side_recv):
    dom, rep = lax.axis_index("dom"), lax.axis_index("rep")
    sib = 1 - rep
    arrive = meet_all(dom, rep, True)
    pack(dom, pick, mixed, outbox)
    wbox[0] = w1[...]
    wbox[1] = jnp.concatenate([w2[...].astype(F32), jnp.zeros((BLK - CLS, BLK), F32)], axis=0).astype(BF16)
    arrive()

    def half(k):
        return pl.ds(pl.multiple_of(k * 64, 64), 64)

    def main(i, s):
        return send_copy(dom, rep, i, outbox, table.at[pl.ds(NB + 2 * s, 2), half(rep)], send_sem, recv_sem)

    def to_sibling(a, b, send, recv):
        return pltpu.make_async_remote_copy(src_ref=a, dst_ref=b, send_sem=send, recv_sem=recv,
                                            device_id=(dom, sib), device_id_type=MESH)

    def passed(i, k):
        part = table.at[pl.ds(NB + 2 * shifted(dom, i, -1), 2), half(k)]
        return to_sibling(part, part, fsend_sem.at[i], frecv_sem.at[i])

    @pl.loop(1, DOM)
    def _(step):
        main(shift_of(step), dom).start()

    weights = to_sibling(wbox, wgot, side_send.at[0], side_recv.at[0])
    own = to_sibling(mixed, table.at[pl.ds(0, NB), half(rep)], side_send.at[1], side_recv.at[1])
    weights.start()
    own.start()

    @pl.loop(0, NB)
    def _(b):
        table[b, half(rep)] = mixed[b]

    weights.wait()
    w1_all[:, :BLK] = wbox[0]
    w1_all[:, BLK:] = wgot[0]
    w2_all[:, :BLK] = wbox[1][:CPAD]
    w2_all[:, BLK:] = wgot[1][:CPAD]
    own.wait_send()
    to_sibling(mixed, table.at[pl.ds(0, NB), half(sib)], side_send.at[1], side_recv.at[1]).wait_recv()

    def activate(e):
        hidden[e] = jnp.maximum(dot(table[e], w1_all[...], TN), 0.0).astype(BF16)

    @pl.loop(0, NB // UNROLL)
    def _(g):
        for u in range(UNROLL):
            activate(g * UNROLL + u)

    def take(g):
        for u in range(BATCH):
            i = shift_of(g * BATCH + u + 1)
            main(i, shifted(dom, i, -1)).wait_recv()
            passed(i, rep).start()

    def finish(g):
        shifts = [shift_of(g * BATCH + u + 1) for u in range(BATCH)]
        for i in shifts:
            main(i, dom).wait_send()
            passed(i, rep).wait_send()
            passed(i, sib).wait_recv()
        for i in shifts:
            e = NB + 2 * shifted(dom, i, -1)
            activate(e)
            activate(e + 1)

    take(0)

    @pl.loop(1, (DOM - 1) // BATCH)
    def _(g):
        take(g)
        finish(g - 1)

    finish((DOM - 1) // BATCH - 1)


def exchange_mixed(pick, mixed, w1, w2):
    return pl.pallas_call(
        mixed_kernel,
        out_shape=(
            jax.ShapeDtypeStruct((ENTRIES, BLK, BLK), BF16),
            jax.ShapeDtypeStruct((ENTRIES, BLK, 2 * BLK), BF16),
            jax.ShapeDtypeStruct((CPAD, 2 * BLK), BF16),
        ),
        in_specs=[SM, VM, VM, VM],
        out_specs=(VM, VM, VM),
        scratch_shapes=[
            pltpu.VMEM((DOM, 2, 64, BLK), BF16),
            pltpu.VMEM((BLK, 2 * BLK), BF16),
            pltpu.VMEM((2, BLK, BLK), BF16),
            pltpu.VMEM((2, BLK, BLK), BF16),
        ] + [pltpu.SemaphoreType.DMA((DOM,))] * 4 + [pltpu.SemaphoreType.DMA((2,))] * 2,
        cost_estimate=COST,
        compiler_params=pltpu.CompilerParams(collective_id=1, has_side_effects=True, vmem_limit_bytes=12 << 20),
    )(pick, mixed, w1, w2)


def build_list(src, dst, first, lists):
    def step(t, count):
        d = dst[t] - first
        lists[0, count] = t
        lists[1, count] = src[t]
        lists[2, count] = d
        return count + jnp.where((d >= 0) & (d < HALF), 1, 0)

    count = lax.fori_loop(NB, NT, step, 0, unroll=8)
    for u in range(UNROLL):
        lists[0, count + u] = 0
        lists[1, count + u] = 0
        lists[2, count + u] = HALF
    return (count + UNROLL - 1) // UNROLL


def sum_first(first, tiles, table, acc, dims):
    @pl.loop(0, HALF // UNROLL)
    def _(g):
        for u in range(UNROLL):
            b = g * UNROLL + u
            acc[b] = dot(tiles[first + b], table[first + b], dims)


def sum_rest(groups, lists, tiles, table, acc, dims):
    @pl.loop(0, groups)
    def _(g):
        for u in range(UNROLL):
            n = g * UNROLL + u
            acc[lists[2, n]] += dot(tiles[lists[0, n]], table[lists[1, n]], dims)


def second_kernel(scale, src_in, dst_in, labels, tiles, table, hidden, w2, pay, hidden_out, src, dst, acc, grad, lists, sem,
                  load_sem):
    first = lax.axis_index("rep") * HALF
    loads = [pltpu.make_async_copy(a, b, load_sem.at[n]) for n, (a, b) in enumerate([(src_in, src), (dst_in, dst)])]
    for load in loads:
        load.start()
    out = pltpu.make_async_copy(hidden.at[pl.ds(0, NB), :, pl.ds(0, BLK)], hidden_out, sem)
    out.start()
    sum_first(first, tiles, hidden, acc, NN)
    for load in loads:
        load.wait()
    groups = build_list(src, dst, first, lists)
    sum_rest(groups, lists, tiles, hidden, acc, NN)
    pay[...] = jnp.zeros_like(pay)
    grad[HALF] = jnp.zeros((BLK, 2 * BLK), BF16)
    w2_t = w2[...]
    kinds = lax.broadcasted_iota(jnp.int32, (CPAD, ROWS), 0)

    def classify(g, loss):
        at = pl.ds(g * WIDE, WIDE)
        second = acc[at].reshape(ROWS, 2 * BLK).astype(BF16)
        logits = dot(w2_t, second, NTR)
        powers = jnp.where(kinds < CLS, jnp.exp(logits), 0.0)
        total = jnp.sum(powers, axis=0, keepdims=True)
        hot = kinds == labels[lax.axis_index("rep") * (HALF // WIDE) + g]
        loss = loss + jnp.log(total) - jnp.sum(jnp.where(hot, logits, 0.0), axis=0, keepdims=True)
        grad_logits = ((powers * (1.0 / total) - jnp.where(hot, 1.0, 0.0)) * scale).astype(BF16)
        pay[BLK:BLK + CPAD] += dot(grad_logits, second, NN)
        grad[at] = dot(grad_logits, w2_t, TN).astype(BF16).reshape(WIDE, BLK, 2 * BLK)
        return loss

    loss = lax.fori_loop(0, HALF // WIDE, classify, jnp.zeros((1, ROWS), F32))
    pay[BLK + CPAD:] = jnp.zeros((PAY - BLK - CPAD, 2 * BLK), F32) + jnp.sum(loss)

    def back(t, e, d):
        part = dot(tiles[t], grad[d], TN).astype(BF16)
        return jnp.where(hidden[e] > 0, part, jnp.zeros_like(part))

    def add_all(at):
        masked = jnp.concatenate([back(*each) for each in at], axis=0)
        rows = jnp.concatenate([table[each[1]] for each in at], axis=1)
        pay[:BLK] += dot(rows, masked, NN)

    @pl.loop(0, HALF // UNROLL)
    def _(g):
        at = [g * UNROLL + u for u in range(UNROLL)]
        add_all([(first + b, first + b, b) for b in at])

    @pl.loop(0, groups)
    def _(g):
        at = [g * UNROLL + u for u in range(UNROLL)]
        add_all([(lists[0, n], lists[1, n], lists[2, n]) for n in at])

    out.wait()


def second_layer(scale, src, dst, labels, tiles, table, hidden, w2):
    return pl.pallas_call(
        functools.partial(second_kernel, scale),
        out_shape=(
            jax.ShapeDtypeStruct((PAY, 2 * BLK), F32),
            jax.ShapeDtypeStruct((NB, BLK, BLK), BF16),
        ),
        in_specs=[ANY, ANY, VM, VM, VM, VM, VM],
        out_specs=(VM, ANY),
        scratch_shapes=[
            pltpu.SMEM((NT,), jnp.int32),
            pltpu.SMEM((NT,), jnp.int32),
            pltpu.VMEM((HALF + 1, BLK, 2 * BLK), F32),
            pltpu.VMEM((HALF + 1, BLK, 2 * BLK), BF16),
            pltpu.SMEM((3, LIST), jnp.int32),
            pltpu.SemaphoreType.DMA(()),
            pltpu.SemaphoreType.DMA((2,)),
        ],
        cost_estimate=COST,
        compiler_params=pltpu.CompilerParams(vmem_limit_bytes=12 << 20),
    )(src, dst, labels, tiles, table, hidden, w2)


def sum_kernel(pay, out, parts, zs, ys, first, second, send_sem, recv_sem):
    dom, rep = lax.axis_index("dom"), lax.axis_index("rep")
    x, z, y = coords(dom)
    sib = 1 - rep
    cores = (rep, sib)

    def along_x(j):
        return lax.rem(x + j, 4)

    def x_peer(j):
        return along_x(j) * 16 + z * 4 + y

    def z_peer(j):
        return x * 16 + lax.rem(z + j, 4) * 4 + y

    def y_peer(j):
        return x * 16 + z * 4 + lax.rem(y + j, 4)

    barrier = pltpu.get_barrier_semaphore()
    peers = [(dom, sib)] + [(x_peer(j), c) for j in range(1, 4) for c in cores]
    peers += [(f(j), rep) for j in range(1, 4) for f in (z_peer, y_peer)]
    for peer in peers:
        pl.semaphore_signal(barrier, inc=1, device_id=peer, device_id_type=MESH)
    pl.semaphore_wait(barrier, len(peers))

    def copy(a, b, n, to):
        return pltpu.make_async_remote_copy(src_ref=a, dst_ref=b, send_sem=send_sem.at[n], recv_sem=recv_sem.at[n],
                                            device_id=to, device_id_type=MESH)

    def rows(k):
        return pl.ds(pl.multiple_of(k * PART, 8), PART)

    cut = []
    for j in (2, 1, 3, 0):
        for k in (1, 0):
            if j or k:
                cut.append(copy(pay.at[rows(along_x(j)), pl.ds(k * BLK, BLK)], parts.at[k, j], 4 * k + j,
                                (x_peer(j), cores[k])))
                cut[-1].start()
    total = pay[rows(x), :BLK]
    for c in cut:
        c.wait()
    for j in range(4):
        for k in range(2):
            if j or k:
                total = total + parts[k, j]
    first[...] = total

    def sum_over(mine, got, n, peer):
        sent = [copy(mine, got.at[j], n + j, (peer(j), rep)) for j in (2, 1, 3)]
        for c in sent:
            c.start()
        for c in sent:
            c.wait()
        return mine[...] + got[1] + got[2] + got[3]

    second[...] = sum_over(first, zs, 8, z_peer)
    out[rows(x)] = sum_over(second, ys, 12, y_peer)

    here = out.at[rows(x)]
    back = [copy(here, here, 16 + j, (x_peer(j), rep)) for j in (2, 1, 3)]
    for c in back:
        c.start()
    for j in (2, 1, 3):
        there = out.at[rows(along_x(4 - j))]
        copy(there, there, 16 + j, (x_peer(j), rep)).wait_recv()
    for c in back:
        c.wait_send()


def sum_all(pay):
    return pl.pallas_call(
        sum_kernel,
        out_shape=jax.ShapeDtypeStruct((PAY, BLK), F32),
        in_specs=[VM],
        out_specs=VM,
        scratch_shapes=[
            pltpu.VMEM((2, 4, PART, BLK), F32),
            pltpu.VMEM((4, PART, BLK), F32),
            pltpu.VMEM((4, PART, BLK), F32),
            pltpu.VMEM((PART, BLK), F32),
            pltpu.VMEM((PART, BLK), F32),
            pltpu.SemaphoreType.DMA((20,)),
            pltpu.SemaphoreType.DMA((20,)),
        ],
        cost_estimate=COST,
        compiler_params=pltpu.CompilerParams(collective_id=2, has_side_effects=True, vmem_limit_bytes=8 << 20),
    )(pay)


def per_device(features, weight_first, weight_second, labels, send_index, tile_src, tile_dst, tile_values):
    node_count = lax.axis_size("dom") * NB * BLK
    pick = send_index[0].T
    table = exchange_features(pick, features.T)
    mixed = first_aggregate(tile_src, tile_dst, tile_values, table)
    mixed_table, hidden, w2 = exchange_mixed(pick, mixed, weight_first, weight_second.T)
    pay, hidden_out = second_layer(
        1.0 / node_count**0.5, tile_src, tile_dst, labels.reshape(NB // WIDE, 1, ROWS), tile_values, mixed_table,
        hidden, w2)
    total = sum_all(pay)
    loss = total[BLK + CPAD, 0] / node_count
    return hidden_out.reshape(NB * BLK, BLK), total[:BLK], total[BLK:BLK + CLS].T, loss


def solution(mesh):
    return jax.shard_map(
        per_device,
        mesh=mesh,
        in_specs=(P("dom", "rep"), P(None, "rep"), P("rep", None), P("dom"), P("dom", None, None), P("dom"), P("dom"),
                  P("dom", None, None)),
        out_specs=(P("dom", "rep"), P(None, "rep"), P("rep", None), P()),
        check_vma=False,
    )
```

```python
import functools

import jax
import jax.numpy as jnp
from jax import lax
from jax.experimental import pallas as pl
from jax.experimental.pallas import tpu as pltpu
from jax.sharding import PartitionSpec as P

MESH = pl.DeviceIdType.MESH
BLK = 128
NB = 64
HALF = NB // 2
S = 2
DOM = 64
NT = 256
ENTRIES = NB + DOM * S
CLS = 47
CPAD = 48
UNROLL = 16
BATCH = 3
MANY = 32
WIDE = 8
ROWS = WIDE * BLK
LIST = NT + UNROLL
PAY = 192
PART = PAY // 4
F32 = jnp.float32
BF16 = jnp.bfloat16

VM = pl.BlockSpec(memory_space=pltpu.VMEM)
SM = pl.BlockSpec(memory_space=pltpu.SMEM)
ANY = pl.BlockSpec(memory_space=pl.ANY)
COST = pl.CostEstimate(flops=10**10, bytes_accessed=10**8, transcendentals=0)


def coords(dom):
    return lax.div(dom, 16), lax.rem(lax.div(dom, 4), 4), lax.rem(dom, 4)


def shifted(dom, i, sign):
    x, z, y = coords(dom)
    dx, dz, dy = coords(i)
    return (lax.rem(x + sign * dx + 4, 4) * 16 + lax.rem(z + sign * dz + 4, 4) * 4 + lax.rem(y + sign * dy + 4, 4))


def shift_of(step):
    return lax.rem(step * 10, 63) + 1


def hops(i):
    return sum(min(d, 4 - d) for d in (i // 16, i // 4 % 4, i % 4))


def meet_all(dom, rep, sibling):
    barrier = pltpu.get_barrier_semaphore()
    x, z, y = coords(dom)
    xs = [lax.rem(x + d, 4) * 16 for d in range(4)]
    zs = [lax.rem(z + d, 4) * 4 for d in range(4)]
    ys = [lax.rem(y + d, 4) for d in range(4)]
    for i in sorted(range(1, DOM), key=lambda i: -hops(i)):
        peer = xs[i // 16] + zs[i // 4 % 4] + ys[i % 4]
        pl.semaphore_signal(barrier, inc=1, device_id=(peer, rep), device_id_type=MESH)
    if sibling:
        pl.semaphore_signal(barrier, inc=1, device_id=(dom, 1 - rep), device_id_type=MESH)
    return lambda: pl.semaphore_wait(barrier, DOM if sibling else DOM - 1)


def dot(a, b, dims):
    return lax.dot_general(a, b, (dims, ((), ())), preferred_element_type=F32)


NN = ((1,), (0,))
TN = ((0,), (0,))
NTR = ((1,), (1,))


def send_copy(dom, rep, i, outbox, landing, send_sem, recv_sem):
    return pltpu.make_async_remote_copy(
        src_ref=outbox.at[i], dst_ref=landing, send_sem=send_sem.at[i], recv_sem=recv_sem.at[i],
        device_id=(shifted(dom, i, 1), rep), device_id_type=MESH)


def pack(dom, pick, blocks, outbox):
    @pl.loop(1, DOM)
    def _(step):
        i = shift_of(step)
        r = shifted(dom, i, 1)
        outbox[i, 0] = blocks[jnp.maximum(pick[0, r], 0)]
        outbox[i, 1] = blocks[jnp.maximum(pick[1, r], 0)]


def feature_kernel(pick, feat, table, blocks, outbox, send_sem, recv_sem):
    dom, rep = lax.axis_index("dom"), lax.axis_index("rep")
    arrive = meet_all(dom, rep, False)

    @pl.loop(0, NB)
    def _(b):
        blocks[b] = feat[:, pl.ds(pl.multiple_of(b * BLK, BLK), BLK)]

    pack(dom, pick, blocks, outbox)
    arrive()

    def main(i, s):
        return send_copy(dom, rep, i, outbox, table.at[pl.ds(NB + 2 * s, 2)], send_sem, recv_sem)

    @pl.loop(1, DOM)
    def _(step):
        main(shift_of(step), dom).start()

    @pl.loop(0, NB)
    def _(b):
        table[b] = blocks[b]

    @pl.loop(1, DOM)
    def _(step):
        i = shift_of(step)
        main(i, shifted(dom, i, -1)).wait_recv()
        main(i, dom).wait_send()


def exchange_features(pick, feat):
    return pl.pallas_call(
        feature_kernel,
        out_shape=jax.ShapeDtypeStruct((ENTRIES, 64, BLK), BF16),
        in_specs=[SM, VM],
        out_specs=VM,
        scratch_shapes=[
            pltpu.VMEM((NB, 64, BLK), BF16),
            pltpu.VMEM((DOM, 2, 64, BLK), BF16),
        ] + [pltpu.SemaphoreType.DMA((DOM,))] * 2,
        cost_estimate=COST,
        compiler_params=pltpu.CompilerParams(collective_id=0, has_side_effects=True, vmem_limit_bytes=12 << 20),
    )(pick, feat)


def first_kernel(src_in, dst_in, tiles, table, mixed, src, dst, acc, load_sem):
    pairs = [(src_in, src), (dst_in, dst)]
    loads = [pltpu.make_async_copy(a, b, load_sem.at[n]) for n, (a, b) in enumerate(pairs)]
    for load in loads:
        load.start()

    @pl.loop(0, NB // MANY)
    def _(g):
        for u in range(MANY):
            b = g * MANY + u
            acc[b] = dot(table[b], tiles[b], NTR)

    for load in loads:
        load.wait()

    @pl.loop(NB // MANY, NT // MANY)
    def _(g):
        for u in range(MANY):
            t = g * MANY + u
            acc[dst[t]] += dot(table[src[t]], tiles[t], NTR)

    @pl.loop(0, NB // MANY)
    def _(g):
        at = pl.ds(g * MANY, MANY)
        mixed[at] = acc[at].astype(BF16)


def first_aggregate(src, dst, tiles, table):
    return pl.pallas_call(
        first_kernel,
        out_shape=jax.ShapeDtypeStruct((NB, 64, BLK), BF16),
        in_specs=[ANY, ANY, VM, VM],
        out_specs=VM,
        scratch_shapes=[
            pltpu.SMEM((NT,), jnp.int32),
            pltpu.SMEM((NT,), jnp.int32),
            pltpu.VMEM((NB, 64, BLK), F32),
            pltpu.SemaphoreType.DMA((2,)),
        ],
        cost_estimate=COST,
        compiler_params=pltpu.CompilerParams(vmem_limit_bytes=14 << 20),
    )(src, dst, tiles, table)


def mixed_kernel(pick, mixed, w1, w2, table, hidden, w2_all, outbox, w1_all, wbox, wgot,
                 send_sem, recv_sem, fsend_sem, frecv_sem, side_send, side_recv):
    dom, rep = lax.axis_index("dom"), lax.axis_index("rep")
    sib = 1 - rep
    arrive = meet_all(dom, rep, True)
    pack(dom, pick, mixed, outbox)
    wbox[0] = w1[...]
    wbox[1] = jnp.concatenate([w2[...].astype(F32), jnp.zeros((BLK - CLS, BLK), F32)], axis=0).astype(BF16)
    arrive()

    def half(k):
        return pl.ds(pl.multiple_of(k * 64, 64), 64)

    def main(i, s):
        return send_copy(dom, rep, i, outbox, table.at[pl.ds(NB + 2 * s, 2), half(rep)], send_sem, recv_sem)

    def to_sibling(a, b, send, recv):
        return pltpu.make_async_remote_copy(src_ref=a, dst_ref=b, send_sem=send, recv_sem=recv,
                                            device_id=(dom, sib), device_id_type=MESH)

    def passed(i, k):
        part = table.at[pl.ds(NB + 2 * shifted(dom, i, -1), 2), half(k)]
        return to_sibling(part, part, fsend_sem.at[i], frecv_sem.at[i])

    @pl.loop(1, DOM)
    def _(step):
        main(shift_of(step), dom).start()

    weights = to_sibling(wbox, wgot, side_send.at[0], side_recv.at[0])
    own = to_sibling(mixed, table.at[pl.ds(0, NB), half(rep)], side_send.at[1], side_recv.at[1])
    weights.start()
    own.start()

    @pl.loop(0, NB)
    def _(b):
        table[b, half(rep)] = mixed[b]

    weights.wait()
    w1_all[:, :BLK] = wbox[0]
    w1_all[:, BLK:] = wgot[0]
    w2_all[:, :BLK] = wbox[1][:CPAD]
    w2_all[:, BLK:] = wgot[1][:CPAD]
    own.wait_send()
    to_sibling(mixed, table.at[pl.ds(0, NB), half(sib)], side_send.at[1], side_recv.at[1]).wait_recv()

    def activate(e):
        hidden[e] = jnp.maximum(dot(table[e], w1_all[...], TN), 0.0).astype(BF16)

    @pl.loop(0, NB // UNROLL)
    def _(g):
        for u in range(UNROLL):
            activate(g * UNROLL + u)

    def take(g):
        for u in range(BATCH):
            i = shift_of(g * BATCH + u + 1)
            main(i, shifted(dom, i, -1)).wait_recv()
            passed(i, rep).start()

    def finish(g):
        shifts = [shift_of(g * BATCH + u + 1) for u in range(BATCH)]
        for i in shifts:
            main(i, dom).wait_send()
            passed(i, rep).wait_send()
            passed(i, sib).wait_recv()
        for i in shifts:
            e = NB + 2 * shifted(dom, i, -1)
            activate(e)
            activate(e + 1)

    @pl.loop(0, 2)
    def _(g):
        take(g)

    @pl.loop(2, (DOM - 1) // BATCH)
    def _(g):
        take(g)
        finish(g - 2)

    finish((DOM - 1) // BATCH - 2)
    finish((DOM - 1) // BATCH - 1)


def exchange_mixed(pick, mixed, w1, w2):
    return pl.pallas_call(
        mixed_kernel,
        out_shape=(
            jax.ShapeDtypeStruct((ENTRIES, BLK, BLK), BF16),
            jax.ShapeDtypeStruct((ENTRIES, BLK, 2 * BLK), BF16),
            jax.ShapeDtypeStruct((CPAD, 2 * BLK), BF16),
        ),
        in_specs=[SM, VM, VM, VM],
        out_specs=(VM, VM, VM),
        scratch_shapes=[
            pltpu.VMEM((DOM, 2, 64, BLK), BF16),
            pltpu.VMEM((BLK, 2 * BLK), BF16),
            pltpu.VMEM((2, BLK, BLK), BF16),
            pltpu.VMEM((2, BLK, BLK), BF16),
        ] + [pltpu.SemaphoreType.DMA((DOM,))] * 4 + [pltpu.SemaphoreType.DMA((2,))] * 2,
        cost_estimate=COST,
        compiler_params=pltpu.CompilerParams(collective_id=1, has_side_effects=True, vmem_limit_bytes=12 << 20),
    )(pick, mixed, w1, w2)


def build_list(src, dst, first, lists):
    def step(t, count):
        d = dst[t] - first
        lists[0, count] = t
        lists[1, count] = src[t]
        lists[2, count] = d
        return count + jnp.where((d >= 0) & (d < HALF), 1, 0)

    count = lax.fori_loop(NB, NT, step, 0, unroll=8)
    for u in range(UNROLL):
        lists[0, count + u] = 0
        lists[1, count + u] = 0
        lists[2, count + u] = HALF
    return (count + UNROLL - 1) // UNROLL


def sum_first(first, tiles, table, acc, dims):
    @pl.loop(0, HALF // UNROLL)
    def _(g):
        for u in range(UNROLL):
            b = g * UNROLL + u
            acc[b] = dot(tiles[first + b], table[first + b], dims)


def sum_rest(groups, lists, tiles, table, acc, dims):
    @pl.loop(0, groups)
    def _(g):
        for u in range(UNROLL):
            n = g * UNROLL + u
            acc[lists[2, n]] += dot(tiles[lists[0, n]], table[lists[1, n]], dims)


def second_kernel(scale, src_in, dst_in, labels, tiles, table, hidden, w2, pay, hidden_out, src, dst, acc, grad, lists, sem,
                  load_sem):
    first = lax.axis_index("rep") * HALF
    loads = [pltpu.make_async_copy(a, b, load_sem.at[n]) for n, (a, b) in enumerate([(src_in, src), (dst_in, dst)])]
    for load in loads:
        load.start()
    out = pltpu.make_async_copy(hidden.at[pl.ds(0, NB), :, pl.ds(0, BLK)], hidden_out, sem)
    out.start()
    sum_first(first, tiles, hidden, acc, NN)
    for load in loads:
        load.wait()
    groups = build_list(src, dst, first, lists)
    sum_rest(groups, lists, tiles, hidden, acc, NN)
    pay[...] = jnp.zeros_like(pay)
    grad[HALF] = jnp.zeros((BLK, 2 * BLK), BF16)
    w2_t = w2[...]
    kinds = lax.broadcasted_iota(jnp.int32, (CPAD, ROWS), 0)

    def classify(g, loss):
        at = pl.ds(g * WIDE, WIDE)
        second = acc[at].reshape(ROWS, 2 * BLK).astype(BF16)
        logits = dot(w2_t, second, NTR)
        powers = jnp.where(kinds < CLS, jnp.exp(logits), 0.0)
        total = jnp.sum(powers, axis=0, keepdims=True)
        hot = kinds == labels[lax.axis_index("rep") * (HALF // WIDE) + g]
        loss = loss + jnp.log(total) - jnp.sum(jnp.where(hot, logits, 0.0), axis=0, keepdims=True)
        grad_logits = ((powers * (1.0 / total) - jnp.where(hot, 1.0, 0.0)) * scale).astype(BF16)
        pay[BLK:BLK + CPAD] += dot(grad_logits, second, NN)
        grad[at] = dot(grad_logits, w2_t, TN).astype(BF16).reshape(WIDE, BLK, 2 * BLK)
        return loss

    loss = lax.fori_loop(0, HALF // WIDE, classify, jnp.zeros((1, ROWS), F32))
    pay[BLK + CPAD:] = jnp.zeros((PAY - BLK - CPAD, 2 * BLK), F32) + jnp.sum(loss)

    def back(t, e, d):
        part = dot(tiles[t], grad[d], TN).astype(BF16)
        return jnp.where(hidden[e] > 0, part, jnp.zeros_like(part))

    def add_all(at):
        masked = jnp.concatenate([back(*each) for each in at], axis=0)
        rows = jnp.concatenate([table[each[1]] for each in at], axis=1)
        pay[:BLK] += dot(rows, masked, NN)

    @pl.loop(0, HALF // UNROLL)
    def _(g):
        at = [g * UNROLL + u for u in range(UNROLL)]
        add_all([(first + b, first + b, b) for b in at])

    @pl.loop(0, groups)
    def _(g):
        at = [g * UNROLL + u for u in range(UNROLL)]
        add_all([(lists[0, n], lists[1, n], lists[2, n]) for n in at])

    out.wait()


def second_layer(scale, src, dst, labels, tiles, table, hidden, w2):
    return pl.pallas_call(
        functools.partial(second_kernel, scale),
        out_shape=(
            jax.ShapeDtypeStruct((PAY, 2 * BLK), F32),
            jax.ShapeDtypeStruct((NB, BLK, BLK), BF16),
        ),
        in_specs=[ANY, ANY, VM, VM, VM, VM, VM],
        out_specs=(VM, ANY),
        scratch_shapes=[
            pltpu.SMEM((NT,), jnp.int32),
            pltpu.SMEM((NT,), jnp.int32),
            pltpu.VMEM((HALF + 1, BLK, 2 * BLK), F32),
            pltpu.VMEM((HALF + 1, BLK, 2 * BLK), BF16),
            pltpu.SMEM((3, LIST), jnp.int32),
            pltpu.SemaphoreType.DMA(()),
            pltpu.SemaphoreType.DMA((2,)),
        ],
        cost_estimate=COST,
        compiler_params=pltpu.CompilerParams(vmem_limit_bytes=12 << 20),
    )(src, dst, labels, tiles, table, hidden, w2)


def sum_kernel(pay, out, parts, zs, ys, first, second, send_sem, recv_sem):
    dom, rep = lax.axis_index("dom"), lax.axis_index("rep")
    x, z, y = coords(dom)
    sib = 1 - rep
    cores = (rep, sib)

    def along_x(j):
        return lax.rem(x + j, 4)

    def x_peer(j):
        return along_x(j) * 16 + z * 4 + y

    def z_peer(j):
        return x * 16 + lax.rem(z + j, 4) * 4 + y

    def y_peer(j):
        return x * 16 + z * 4 + lax.rem(y + j, 4)

    barrier = pltpu.get_barrier_semaphore()
    peers = [(dom, sib)] + [(x_peer(j), c) for j in range(1, 4) for c in cores]
    peers += [(f(j), rep) for j in range(1, 4) for f in (z_peer, y_peer)]
    for peer in peers:
        pl.semaphore_signal(barrier, inc=1, device_id=peer, device_id_type=MESH)
    pl.semaphore_wait(barrier, len(peers))

    def copy(a, b, n, to):
        return pltpu.make_async_remote_copy(src_ref=a, dst_ref=b, send_sem=send_sem.at[n], recv_sem=recv_sem.at[n],
                                            device_id=to, device_id_type=MESH)

    def rows(k):
        return pl.ds(pl.multiple_of(k * PART, 8), PART)

    cut = []
    for j in (2, 1, 3, 0):
        for k in (1, 0):
            if j or k:
                cut.append(copy(pay.at[rows(along_x(j)), pl.ds(k * BLK, BLK)], parts.at[k, j], 4 * k + j,
                                (x_peer(j), cores[k])))
                cut[-1].start()
    total = pay[rows(x), :BLK]
    for c in cut:
        c.wait()
    for j in range(4):
        for k in range(2):
            if j or k:
                total = total + parts[k, j]
    first[...] = total

    def sum_over(mine, got, n, peer):
        sent = [copy(mine, got.at[j], n + j, (peer(j), rep)) for j in (2, 1, 3)]
        for c in sent:
            c.start()
        for c in sent:
            c.wait()
        return mine[...] + got[1] + got[2] + got[3]

    second[...] = sum_over(first, zs, 8, z_peer)
    out[rows(x)] = sum_over(second, ys, 12, y_peer)

    here = out.at[rows(x)]
    back = [copy(here, here, 16 + j, (x_peer(j), rep)) for j in (2, 1, 3)]
    for c in back:
        c.start()
    for j in (2, 1, 3):
        there = out.at[rows(along_x(4 - j))]
        copy(there, there, 16 + j, (x_peer(j), rep)).wait_recv()
    for c in back:
        c.wait_send()


def sum_all(pay):
    return pl.pallas_call(
        sum_kernel,
        out_shape=jax.ShapeDtypeStruct((PAY, BLK), F32),
        in_specs=[VM],
        out_specs=VM,
        scratch_shapes=[
            pltpu.VMEM((2, 4, PART, BLK), F32),
            pltpu.VMEM((4, PART, BLK), F32),
            pltpu.VMEM((4, PART, BLK), F32),
            pltpu.VMEM((PART, BLK), F32),
            pltpu.VMEM((PART, BLK), F32),
            pltpu.SemaphoreType.DMA((20,)),
            pltpu.SemaphoreType.DMA((20,)),
        ],
        cost_estimate=COST,
        compiler_params=pltpu.CompilerParams(collective_id=2, has_side_effects=True, vmem_limit_bytes=8 << 20),
    )(pay)


def per_device(features, weight_first, weight_second, labels, send_index, tile_src, tile_dst, tile_values):
    node_count = lax.axis_size("dom") * NB * BLK
    pick = send_index[0].T
    table = exchange_features(pick, features.T)
    mixed = first_aggregate(tile_src, tile_dst, tile_values, table)
    mixed_table, hidden, w2 = exchange_mixed(pick, mixed, weight_first, weight_second.T)
    pay, hidden_out = second_layer(
        1.0 / node_count**0.5, tile_src, tile_dst, labels.reshape(NB // WIDE, 1, ROWS), tile_values, mixed_table,
        hidden, w2)
    total = sum_all(pay)
    loss = total[BLK + CPAD, 0] / node_count
    return hidden_out.reshape(NB * BLK, BLK), total[:BLK], total[BLK:BLK + CLS].T, loss


def solution(mesh):
    return jax.shard_map(
        per_device,
        mesh=mesh,
        in_specs=(P("dom", "rep"), P(None, "rep"), P("rep", None), P("dom"), P("dom", None, None), P("dom"), P("dom"),
                  P("dom", None, None)),
        out_specs=(P("dom", "rep"), P(None, "rep"), P("rep", None), P()),
        check_vma=False,
    )
```

```python
import functools

import jax
import jax.numpy as jnp
from jax import lax
from jax.experimental import pallas as pl
from jax.experimental.pallas import tpu as pltpu
from jax.sharding import PartitionSpec as P

MESH = pl.DeviceIdType.MESH
BLK = 128
NB = 64
HALF = NB // 2
S = 2
DOM = 64
NT = 256
ENTRIES = NB + DOM * S
CLS = 47
CPAD = 48
UNROLL = 16
BATCH = 3
MANY = 64
WIDE = 8
ROWS = WIDE * BLK
LIST = NT + UNROLL
PAY = 192
PART = PAY // 4
F32 = jnp.float32
BF16 = jnp.bfloat16

VM = pl.BlockSpec(memory_space=pltpu.VMEM)
SM = pl.BlockSpec(memory_space=pltpu.SMEM)
ANY = pl.BlockSpec(memory_space=pl.ANY)
COST = pl.CostEstimate(flops=10**10, bytes_accessed=10**8, transcendentals=0)


def coords(dom):
    return lax.div(dom, 16), lax.rem(lax.div(dom, 4), 4), lax.rem(dom, 4)


def shifted(dom, i, sign):
    x, z, y = coords(dom)
    dx, dz, dy = coords(i)
    return (lax.rem(x + sign * dx + 4, 4) * 16 + lax.rem(z + sign * dz + 4, 4) * 4 + lax.rem(y + sign * dy + 4, 4))


def shift_of(step):
    return lax.rem(step * 10, 63) + 1


def hops(i):
    return sum(min(d, 4 - d) for d in (i // 16, i // 4 % 4, i % 4))


def meet_all(dom, rep, sibling):
    barrier = pltpu.get_barrier_semaphore()
    x, z, y = coords(dom)
    xs = [lax.rem(x + d, 4) * 16 for d in range(4)]
    zs = [lax.rem(z + d, 4) * 4 for d in range(4)]
    ys = [lax.rem(y + d, 4) for d in range(4)]
    for i in sorted(range(1, DOM), key=lambda i: -hops(i)):
        peer = xs[i // 16] + zs[i // 4 % 4] + ys[i % 4]
        pl.semaphore_signal(barrier, inc=1, device_id=(peer, rep), device_id_type=MESH)
    if sibling:
        pl.semaphore_signal(barrier, inc=1, device_id=(dom, 1 - rep), device_id_type=MESH)
    return lambda: pl.semaphore_wait(barrier, DOM if sibling else DOM - 1)


def dot(a, b, dims):
    return lax.dot_general(a, b, (dims, ((), ())), preferred_element_type=F32)


NN = ((1,), (0,))
TN = ((0,), (0,))
NTR = ((1,), (1,))


def send_copy(dom, rep, i, outbox, landing, send_sem, recv_sem):
    return pltpu.make_async_remote_copy(
        src_ref=outbox.at[i], dst_ref=landing, send_sem=send_sem.at[i], recv_sem=recv_sem.at[i],
        device_id=(shifted(dom, i, 1), rep), device_id_type=MESH)


def pack(dom, pick, blocks, outbox):
    @pl.loop(1, DOM)
    def _(step):
        i = shift_of(step)
        r = shifted(dom, i, 1)
        outbox[i, 0] = blocks[jnp.maximum(pick[0, r], 0)]
        outbox[i, 1] = blocks[jnp.maximum(pick[1, r], 0)]


def feature_kernel(pick, feat, table, blocks, outbox, send_sem, recv_sem):
    dom, rep = lax.axis_index("dom"), lax.axis_index("rep")
    arrive = meet_all(dom, rep, False)

    @pl.loop(0, NB)
    def _(b):
        blocks[b] = feat[:, pl.ds(pl.multiple_of(b * BLK, BLK), BLK)]

    pack(dom, pick, blocks, outbox)
    arrive()

    def main(i, s):
        return send_copy(dom, rep, i, outbox, table.at[pl.ds(NB + 2 * s, 2)], send_sem, recv_sem)

    @pl.loop(1, DOM)
    def _(step):
        main(shift_of(step), dom).start()

    @pl.loop(0, NB)
    def _(b):
        table[b] = blocks[b]

    @pl.loop(1, DOM)
    def _(step):
        i = shift_of(step)
        main(i, shifted(dom, i, -1)).wait_recv()
        main(i, dom).wait_send()


def exchange_features(pick, feat):
    return pl.pallas_call(
        feature_kernel,
        out_shape=jax.ShapeDtypeStruct((ENTRIES, 64, BLK), BF16),
        in_specs=[SM, VM],
        out_specs=VM,
        scratch_shapes=[
            pltpu.VMEM((NB, 64, BLK), BF16),
            pltpu.VMEM((DOM, 2, 64, BLK), BF16),
        ] + [pltpu.SemaphoreType.DMA((DOM,))] * 2,
        cost_estimate=COST,
        compiler_params=pltpu.CompilerParams(collective_id=0, has_side_effects=True, vmem_limit_bytes=12 << 20),
    )(pick, feat)


def first_kernel(src_in, dst_in, tiles, table, mixed, src, dst, acc, load_sem):
    pairs = [(src_in, src), (dst_in, dst)]
    loads = [pltpu.make_async_copy(a, b, load_sem.at[n]) for n, (a, b) in enumerate(pairs)]
    for load in loads:
        load.start()

    @pl.loop(0, NB // MANY)
    def _(g):
        for u in range(MANY):
            b = g * MANY + u
            acc[b] = dot(table[b], tiles[b], NTR)

    for load in loads:
        load.wait()

    @pl.loop(NB // MANY, NT // MANY)
    def _(g):
        for u in range(MANY):
            t = g * MANY + u
            acc[dst[t]] += dot(table[src[t]], tiles[t], NTR)

    @pl.loop(0, NB // MANY)
    def _(g):
        at = pl.ds(g * MANY, MANY)
        mixed[at] = acc[at].astype(BF16)


def first_aggregate(src, dst, tiles, table):
    return pl.pallas_call(
        first_kernel,
        out_shape=jax.ShapeDtypeStruct((NB, 64, BLK), BF16),
        in_specs=[ANY, ANY, VM, VM],
        out_specs=VM,
        scratch_shapes=[
            pltpu.SMEM((NT,), jnp.int32),
            pltpu.SMEM((NT,), jnp.int32),
            pltpu.VMEM((NB, 64, BLK), F32),
            pltpu.SemaphoreType.DMA((2,)),
        ],
        cost_estimate=COST,
        compiler_params=pltpu.CompilerParams(vmem_limit_bytes=14 << 20),
    )(src, dst, tiles, table)


def mixed_kernel(pick, mixed, w1, w2, table, hidden, w2_all, outbox, w1_all, wbox, wgot,
                 send_sem, recv_sem, fsend_sem, frecv_sem, side_send, side_recv):
    dom, rep = lax.axis_index("dom"), lax.axis_index("rep")
    sib = 1 - rep
    arrive = meet_all(dom, rep, True)
    pack(dom, pick, mixed, outbox)
    wbox[0] = w1[...]
    wbox[1] = jnp.concatenate([w2[...].astype(F32), jnp.zeros((BLK - CLS, BLK), F32)], axis=0).astype(BF16)
    arrive()

    def half(k):
        return pl.ds(pl.multiple_of(k * 64, 64), 64)

    def main(i, s):
        return send_copy(dom, rep, i, outbox, table.at[pl.ds(NB + 2 * s, 2), half(rep)], send_sem, recv_sem)

    def to_sibling(a, b, send, recv):
        return pltpu.make_async_remote_copy(src_ref=a, dst_ref=b, send_sem=send, recv_sem=recv,
                                            device_id=(dom, sib), device_id_type=MESH)

    def passed(i, k):
        part = table.at[pl.ds(NB + 2 * shifted(dom, i, -1), 2), half(k)]
        return to_sibling(part, part, fsend_sem.at[i], frecv_sem.at[i])

    @pl.loop(1, DOM)
    def _(step):
        main(shift_of(step), dom).start()

    weights = to_sibling(wbox, wgot, side_send.at[0], side_recv.at[0])
    own = to_sibling(mixed, table.at[pl.ds(0, NB), half(rep)], side_send.at[1], side_recv.at[1])
    weights.start()
    own.start()

    @pl.loop(0, NB)
    def _(b):
        table[b, half(rep)] = mixed[b]

    weights.wait()
    w1_all[:, :BLK] = wbox[0]
    w1_all[:, BLK:] = wgot[0]
    w2_all[:, :BLK] = wbox[1][:CPAD]
    w2_all[:, BLK:] = wgot[1][:CPAD]
    own.wait_send()
    to_sibling(mixed, table.at[pl.ds(0, NB), half(sib)], side_send.at[1], side_recv.at[1]).wait_recv()

    def activate(e):
        hidden[e] = jnp.maximum(dot(table[e], w1_all[...], TN), 0.0).astype(BF16)

    @pl.loop(0, NB // UNROLL)
    def _(g):
        for u in range(UNROLL):
            activate(g * UNROLL + u)

    def take(g):
        for u in range(BATCH):
            i = shift_of(g * BATCH + u + 1)
            main(i, shifted(dom, i, -1)).wait_recv()
            passed(i, rep).start()

    def finish(g):
        shifts = [shift_of(g * BATCH + u + 1) for u in range(BATCH)]
        for i in shifts:
            main(i, dom).wait_send()
            passed(i, rep).wait_send()
            passed(i, sib).wait_recv()
        for i in shifts:
            e = NB + 2 * shifted(dom, i, -1)
            activate(e)
            activate(e + 1)

    @pl.loop(0, 2)
    def _(g):
        take(g)

    @pl.loop(2, (DOM - 1) // BATCH)
    def _(g):
        take(g)
        finish(g - 2)

    finish((DOM - 1) // BATCH - 2)
    finish((DOM - 1) // BATCH - 1)


def exchange_mixed(pick, mixed, w1, w2):
    return pl.pallas_call(
        mixed_kernel,
        out_shape=(
            jax.ShapeDtypeStruct((ENTRIES, BLK, BLK), BF16),
            jax.ShapeDtypeStruct((ENTRIES, BLK, 2 * BLK), BF16),
            jax.ShapeDtypeStruct((CPAD, 2 * BLK), BF16),
        ),
        in_specs=[SM, VM, VM, VM],
        out_specs=(VM, VM, VM),
        scratch_shapes=[
            pltpu.VMEM((DOM, 2, 64, BLK), BF16),
            pltpu.VMEM((BLK, 2 * BLK), BF16),
            pltpu.VMEM((2, BLK, BLK), BF16),
            pltpu.VMEM((2, BLK, BLK), BF16),
        ] + [pltpu.SemaphoreType.DMA((DOM,))] * 4 + [pltpu.SemaphoreType.DMA((2,))] * 2,
        cost_estimate=COST,
        compiler_params=pltpu.CompilerParams(collective_id=1, has_side_effects=True, vmem_limit_bytes=12 << 20),
    )(pick, mixed, w1, w2)


def build_list(src, dst, first, lists):
    def step(t, count):
        d = dst[t] - first
        lists[0, count] = t
        lists[1, count] = src[t]
        lists[2, count] = d
        return count + jnp.where((d >= 0) & (d < HALF), 1, 0)

    count = lax.fori_loop(NB, NT, step, 0, unroll=8)
    for u in range(UNROLL):
        lists[0, count + u] = 0
        lists[1, count + u] = 0
        lists[2, count + u] = HALF
    return (count + UNROLL - 1) // UNROLL


def sum_first(first, tiles, table, acc, dims):
    @pl.loop(0, HALF // UNROLL)
    def _(g):
        for u in range(UNROLL):
            b = g * UNROLL + u
            acc[b] = dot(tiles[first + b], table[first + b], dims)


def sum_rest(groups, lists, tiles, table, acc, dims):
    @pl.loop(0, groups)
    def _(g):
        for u in range(UNROLL):
            n = g * UNROLL + u
            acc[lists[2, n]] += dot(tiles[lists[0, n]], table[lists[1, n]], dims)


def second_kernel(scale, src_in, dst_in, labels, tiles, table, hidden, w2, pay, hidden_out, src, dst, acc, grad, lists, sem,
                  load_sem):
    first = lax.axis_index("rep") * HALF
    loads = [pltpu.make_async_copy(a, b, load_sem.at[n]) for n, (a, b) in enumerate([(src_in, src), (dst_in, dst)])]
    for load in loads:
        load.start()
    out = pltpu.make_async_copy(hidden.at[pl.ds(0, NB), :, pl.ds(0, BLK)], hidden_out, sem)
    out.start()
    sum_first(first, tiles, hidden, acc, NN)
    for load in loads:
        load.wait()
    groups = build_list(src, dst, first, lists)
    sum_rest(groups, lists, tiles, hidden, acc, NN)
    pay[...] = jnp.zeros_like(pay)
    grad[HALF] = jnp.zeros((BLK, 2 * BLK), BF16)
    w2_t = w2[...]
    kinds = lax.broadcasted_iota(jnp.int32, (CPAD, ROWS), 0)

    def classify(g, loss):
        at = pl.ds(g * WIDE, WIDE)
        second = acc[at].reshape(ROWS, 2 * BLK).astype(BF16)
        logits = dot(w2_t, second, NTR)
        powers = jnp.where(kinds < CLS, jnp.exp(logits), 0.0)
        total = jnp.sum(powers, axis=0, keepdims=True)
        hot = kinds == labels[lax.axis_index("rep") * (HALF // WIDE) + g]
        loss = loss + jnp.log(total) - jnp.sum(jnp.where(hot, logits, 0.0), axis=0, keepdims=True)
        grad_logits = ((powers * (1.0 / total) - jnp.where(hot, 1.0, 0.0)) * scale).astype(BF16)
        pay[BLK:BLK + CPAD] += dot(grad_logits, second, NN)
        grad[at] = dot(grad_logits, w2_t, TN).astype(BF16).reshape(WIDE, BLK, 2 * BLK)
        return loss

    loss = lax.fori_loop(0, HALF // WIDE, classify, jnp.zeros((1, ROWS), F32))
    pay[BLK + CPAD:] = jnp.zeros((PAY - BLK - CPAD, 2 * BLK), F32) + jnp.sum(loss)

    def back(t, e, d):
        part = dot(tiles[t], grad[d], TN).astype(BF16)
        return jnp.where(hidden[e] > 0, part, jnp.zeros_like(part))

    def add_all(at):
        masked = jnp.concatenate([back(*each) for each in at], axis=0)
        rows = jnp.concatenate([table[each[1]] for each in at], axis=1)
        pay[:BLK] += dot(rows, masked, NN)

    @pl.loop(0, HALF // UNROLL)
    def _(g):
        at = [g * UNROLL + u for u in range(UNROLL)]
        add_all([(first + b, first + b, b) for b in at])

    @pl.loop(0, groups)
    def _(g):
        at = [g * UNROLL + u for u in range(UNROLL)]
        add_all([(lists[0, n], lists[1, n], lists[2, n]) for n in at])

    out.wait()


def second_layer(scale, src, dst, labels, tiles, table, hidden, w2):
    return pl.pallas_call(
        functools.partial(second_kernel, scale),
        out_shape=(
            jax.ShapeDtypeStruct((PAY, 2 * BLK), F32),
            jax.ShapeDtypeStruct((NB, BLK, BLK), BF16),
        ),
        in_specs=[ANY, ANY, VM, VM, VM, VM, VM],
        out_specs=(VM, ANY),
        scratch_shapes=[
            pltpu.SMEM((NT,), jnp.int32),
            pltpu.SMEM((NT,), jnp.int32),
            pltpu.VMEM((HALF + 1, BLK, 2 * BLK), F32),
            pltpu.VMEM((HALF + 1, BLK, 2 * BLK), BF16),
            pltpu.SMEM((3, LIST), jnp.int32),
            pltpu.SemaphoreType.DMA(()),
            pltpu.SemaphoreType.DMA((2,)),
        ],
        cost_estimate=COST,
        compiler_params=pltpu.CompilerParams(vmem_limit_bytes=12 << 20),
    )(src, dst, labels, tiles, table, hidden, w2)


def sum_kernel(pay, out, parts, zs, ys, first, second, send_sem, recv_sem):
    dom, rep = lax.axis_index("dom"), lax.axis_index("rep")
    x, z, y = coords(dom)
    sib = 1 - rep
    cores = (rep, sib)

    def along_x(j):
        return lax.rem(x + j, 4)

    def x_peer(j):
        return along_x(j) * 16 + z * 4 + y

    def z_peer(j):
        return x * 16 + lax.rem(z + j, 4) * 4 + y

    def y_peer(j):
        return x * 16 + z * 4 + lax.rem(y + j, 4)

    barrier = pltpu.get_barrier_semaphore()
    peers = [(dom, sib)] + [(x_peer(j), c) for j in range(1, 4) for c in cores]
    peers += [(f(j), rep) for j in range(1, 4) for f in (z_peer, y_peer)]
    for peer in peers:
        pl.semaphore_signal(barrier, inc=1, device_id=peer, device_id_type=MESH)
    pl.semaphore_wait(barrier, len(peers))

    def copy(a, b, n, to):
        return pltpu.make_async_remote_copy(src_ref=a, dst_ref=b, send_sem=send_sem.at[n], recv_sem=recv_sem.at[n],
                                            device_id=to, device_id_type=MESH)

    def rows(k):
        return pl.ds(pl.multiple_of(k * PART, 8), PART)

    cut = []
    for j in (2, 1, 3, 0):
        for k in (1, 0):
            if j or k:
                cut.append(copy(pay.at[rows(along_x(j)), pl.ds(k * BLK, BLK)], parts.at[k, j], 4 * k + j,
                                (x_peer(j), cores[k])))
                cut[-1].start()
    total = pay[rows(x), :BLK]
    for c in cut:
        c.wait()
    for j in range(4):
        for k in range(2):
            if j or k:
                total = total + parts[k, j]
    first[...] = total

    def sum_over(mine, got, n, peer):
        sent = [copy(mine, got.at[j], n + j, (peer(j), rep)) for j in (2, 1, 3)]
        for c in sent:
            c.start()
        for c in sent:
            c.wait()
        return mine[...] + got[1] + got[2] + got[3]

    second[...] = sum_over(first, zs, 8, z_peer)
    out[rows(x)] = sum_over(second, ys, 12, y_peer)

    here = out.at[rows(x)]
    back = [copy(here, here, 16 + j, (x_peer(j), rep)) for j in (2, 1, 3)]
    for c in back:
        c.start()
    for j in (2, 1, 3):
        there = out.at[rows(along_x(4 - j))]
        copy(there, there, 16 + j, (x_peer(j), rep)).wait_recv()
    for c in back:
        c.wait_send()


def sum_all(pay):
    return pl.pallas_call(
        sum_kernel,
        out_shape=jax.ShapeDtypeStruct((PAY, BLK), F32),
        in_specs=[VM],
        out_specs=VM,
        scratch_shapes=[
            pltpu.VMEM((2, 4, PART, BLK), F32),
            pltpu.VMEM((4, PART, BLK), F32),
            pltpu.VMEM((4, PART, BLK), F32),
            pltpu.VMEM((PART, BLK), F32),
            pltpu.VMEM((PART, BLK), F32),
            pltpu.SemaphoreType.DMA((20,)),
            pltpu.SemaphoreType.DMA((20,)),
        ],
        cost_estimate=COST,
        compiler_params=pltpu.CompilerParams(collective_id=2, has_side_effects=True, vmem_limit_bytes=8 << 20),
    )(pay)


def per_device(features, weight_first, weight_second, labels, send_index, tile_src, tile_dst, tile_values):
    node_count = lax.axis_size("dom") * NB * BLK
    pick = send_index[0].T
    table = exchange_features(pick, features.T)
    mixed = first_aggregate(tile_src, tile_dst, tile_values, table)
    mixed_table, hidden, w2 = exchange_mixed(pick, mixed, weight_first, weight_second.T)
    pay, hidden_out = second_layer(
        1.0 / node_count**0.5, tile_src, tile_dst, labels.reshape(NB // WIDE, 1, ROWS), tile_values, mixed_table,
        hidden, w2)
    total = sum_all(pay)
    loss = total[BLK + CPAD, 0] / node_count
    return hidden_out.reshape(NB * BLK, BLK), total[:BLK], total[BLK:BLK + CLS].T, loss


def solution(mesh):
    return jax.shard_map(
        per_device,
        mesh=mesh,
        in_specs=(P("dom", "rep"), P(None, "rep"), P("rep", None), P("dom"), P("dom", None, None), P("dom"), P("dom"),
                  P("dom", None, None)),
        out_specs=(P("dom", "rep"), P(None, "rep"), P("rep", None), P()),
        check_vma=False,
    )
```
